256 devices in a mesh: slab: 32 (over z, y), pencil: 8 (over x, core).
Axes of the slice: x: 4, y: 4, z: 8, core: 2. Of those that a mesh axis runs over, the one named last changes fastest.
Arguments:
- activation: bfloat16 [256, 256, 16, 256], P('pencil', 'slab'), may hold values from -6 to 6
- preact: bfloat16 [256, 256, 16, 256], P('pencil', 'slab'), may hold values from -9 to 9
- cotangent: bfloat16 [256, 256, 16, 256], P('pencil', 'slab'), may hold values from -6 to 6
- local_weight: float32 [16, 16], replicated, may hold values from -1.5 to 1.5
- spectral_weight: float32 [32, 32, 32, 2, 256], P('slab', None, 'pencil'), may hold values from -24 to 24
Outputs:
- grad_activation: bfloat16 [256, 256, 16, 256], P('pencil', 'slab')
- grad_local: float32 [16, 16], replicated
- grad_spectral: float32 [32, 32, 32, 2, 256], P('slab', None, 'pencil')
The draws below stay inside these ranges and needn't reach their ends.
All inputs are finite; a program needn't handle non-finite values.
Results may differ from the reference program's by a relative error of at most 0.002.
Values sent between devices are 32-bit elements; how exact they have to be, the bound alone decides.
A program may use at most 192 MiB of HBM per device.

```python
import jax
import jax.numpy as jnp
from jax import lax

GRID = 256
CHAN = 16
MODES = 32


def block_scale(rng, extent, pieces, least, largest):
    def one(dim, shards_of):
        heights = jax.random.uniform(jax.random.fold_in(jax.random.fold_in(rng, 6), dim), (shards_of,), jnp.float32, least / len(pieces), largest / len(pieces))
        return jnp.repeat(jnp.exp(heights), extent[dim] // shards_of).reshape((-1,) + (1,) * (len(extent) - dim - 1))

    level = one(*pieces[0])
    for cut in pieces[1:]:
        level = level * one(*cut)
    return level


def noise(key, extent, deviation, limit, split=(), kind=jnp.bfloat16):
    gain = block_scale(key, extent, split, -0.22, 0.18) if split else 1.0
    result = jax.random.normal(key, extent, jnp.float32) * deviation * gain
    return jnp.minimum(jnp.maximum(result, -limit), limit).astype(kind)


def setup_inputs(seed: int = 0) -> dict:
    streams_of = jax.random.split(jax.random.key(seed), 6)
    return {
        "activation": noise(streams_of[0], (GRID, GRID, CHAN, GRID), 1.0, 6.0, ((0, 8), (1, 32))),
        "preact": noise(streams_of[1], (GRID, GRID, CHAN, GRID), 1.5, 9.0, ((0, 8), (1, 32))),
        "cotangent": noise(streams_of[2], (GRID, GRID, CHAN, GRID), 1.0, 6.0, ((0, 8), (1, 32))),
        "local_weight": noise(streams_of[3], (CHAN, CHAN), CHAN ** -0.5, 1.5, (), jnp.float32),
        "spectral_weight": noise(streams_of[4], (MODES, MODES, MODES, 2, CHAN * CHAN), 4.0, 24.0, ((0, 32), (2, 8)), jnp.float32),
    }


def gelu_slope(value):
    normal_cdf = 0.5 * (1.0 + jax.scipy.special.erf(value * 0.7071067811865476))
    density = jnp.exp(-0.5 * value * value) * 0.3989422804014327
    return normal_cdf + value * density


def kept_index(length):
    order_index = jnp.arange(MODES, dtype=jnp.int32)
    return jnp.where(order_index < MODES // 2, order_index, order_index + length - MODES).astype(jnp.int32)


def field_modes(field, index):
    spectrum = jnp.fft.fftn(field)
    spectrum = jnp.take(spectrum, index, axis=0)
    spectrum = jnp.take(spectrum, index, axis=1)
    spectrum = jnp.take(spectrum, index, axis=2)
    return jnp.transpose(spectrum, (2, 0, 1))


def reference(activation, preact, cotangent, local_weight, spectral_weight):
    highest = lax.Precision.HIGHEST
    g_pre = cotangent.astype(jnp.float32) * gelu_slope(preact.astype(jnp.float32))
    index = kept_index(GRID)
    channel_ids = jnp.arange(CHAN, dtype=jnp.int32)
    cube = float(GRID) ** 3

    def input_modes(channel):
        field = lax.dynamic_index_in_dim(activation, channel, 2, keepdims=False).astype(jnp.float32)
        return field_modes(field, index)

    def gradient_modes(channel):
        field = lax.dynamic_index_in_dim(g_pre, channel, 2, keepdims=False)
        return field_modes(field, index) / cube

    upper = lax.map(input_modes, channel_ids)
    lower = lax.map(gradient_modes, channel_ids)
    shaped = spectral_weight.reshape(MODES, MODES, MODES, 2, CHAN, CHAN)
    weights = lax.complex(shaped[:, :, :, 0], shaped[:, :, :, 1])
    outer = jnp.einsum('oabc,iabc->abcoi', lower, jnp.conj(upper), precision=highest)
    grad_spectral = jnp.stack([jnp.real(outer), jnp.imag(outer)], axis=3).reshape(MODES, MODES, MODES, 2, CHAN * CHAN)
    back = jnp.einsum('abcoi,oabc->iabc', jnp.conj(weights), lower, precision=highest)

    def finish(inputs):
        channel, modes_block = inputs
        column = lax.dynamic_index_in_dim(local_weight, channel, 1, keepdims=False)
        local_part = jnp.einsum('yzox,o->yzx', g_pre, column, precision=highest)
        padded = jnp.zeros((GRID, GRID, GRID), modes_block.dtype)
        padded = padded.at[index[:, None, None], index[None, :, None], index[None, None, :]].set(jnp.transpose(modes_block, (1, 2, 0)))
        spectral_part = jnp.real(jnp.fft.ifftn(padded)) * cube
        return (local_part + spectral_part).astype(jnp.bfloat16)

    per_channel = lax.map(finish, (channel_ids, back))
    grad_activation = jnp.transpose(per_channel, (1, 2, 0, 3))
    grad_local = jnp.einsum('yzox,yzix->oi', g_pre, activation.astype(jnp.float32), precision=highest) * (float(GRID) ** -1.5)
    return grad_activation, grad_local, grad_spectral
```

```python
import functools

import jax
import jax.numpy as jnp
import ml_dtypes
import numpy as np
from jax import lax
from jax.experimental import pallas as pl
from jax.experimental.pallas import tpu as pltpu
from jax.sharding import PartitionSpec as P

GRID = 256
CHAN = 16
MODES = 32
SLABS = 32
PENCILS = 8
ROWS = GRID // PENCILS
PLANES = GRID // SLABS
LANES = PLANES * CHAN
HALF = MODES // 2 + 1
XROWS = 40
XPAD = 48
CORES = 2
CHIPS = PENCILS // CORES
FIRST = 9
REST = HALF - FIRST
EDGE = CHIPS * HALF
BLOCK = EDGE + XROWS // 8
PARTS = 8
MODE_ROWS = 512
CHUNK = 8
LOADS = ((0, 4), (4, 8), (8, 16), (16, 24), (24, 32))
PAIR = 2
F32 = jnp.float32
BF16 = jnp.bfloat16


def kept(j):
    return np.where(j < MODES // 2, j, j - MODES)


def y_set(p):
    if p == 0:
        return np.array([0, 1, -1, -16])
    return np.array([2 * p, 2 * p + 1, -2 * p - 1, -2 * p])


def pieces(table):
    high = table.astype(np.float32).astype(ml_dtypes.bfloat16)
    low = (table - high.astype(np.float64)).astype(np.float32).astype(ml_dtypes.bfloat16)
    return high, low


def turn(freq, position):
    angle = 2.0 * np.pi * ((freq * position) % GRID) / GRID
    return np.cos(angle), np.sin(angle)


@functools.cache
def tables():
    made = {}
    cells = np.arange(GRID)

    cosine, sine = turn(np.arange(HALF)[:, None], cells[None, :])
    forward_x = np.zeros((XPAD, GRID))
    forward_x[:HALF], forward_x[HALF : 2 * HALF] = cosine, -sine
    made["xf"] = np.concatenate(pieces(forward_x), axis=0)
    high, low = pieces(forward_x[:XROWS])
    made["xi"] = np.concatenate([high, high, low, np.zeros((8, GRID), high.dtype)], axis=0)

    forward_y = np.zeros((PENCILS, 80, 2, ROWS))
    inverse_y = np.zeros((PENCILS, 2, ROWS, PENCILS, 2, 4))
    extra_y = np.zeros((PENCILS, 2, ROWS, LANES))
    for p in range(PENCILS):
        rows = p * ROWS + np.arange(ROWS)
        for d in range(PENCILS):
            cosine, sine = turn(y_set(d)[:, None], rows[None, :])
            forward_y[p, 8 * d : 8 * d + 4, 0], forward_y[p, 8 * d : 8 * d + 4, 1] = cosine, sine
            forward_y[p, 8 * d + 4 : 8 * d + 8, 0], forward_y[p, 8 * d + 4 : 8 * d + 8, 1] = -sine, cosine
            inverse_y[p, 0, :, d, 0], inverse_y[p, 0, :, d, 1] = cosine.T, -sine.T
            inverse_y[p, 1, :, d, 0], inverse_y[p, 1, :, d, 1] = sine.T, cosine.T
        cosine, sine = turn(16, rows)
        forward_y[p, 64, 0], forward_y[p, 64, 1] = cosine, sine
        forward_y[p, 65, 0], forward_y[p, 65, 1] = -sine, cosine
        extra_y[p, 0], extra_y[p, 1] = cosine[:, None], sine[:, None]
    high, low = pieces(forward_y.reshape(PENCILS, 80, 2 * ROWS))
    made["yf"] = np.concatenate([high, high, low], axis=2)
    high, low = pieces(inverse_y.reshape(PENCILS, 2 * ROWS, 64))
    made["yi"] = np.concatenate([high, high, low], axis=2)
    made["ye"] = extra_y.astype(np.float32)

    z_freq = kept(np.arange(MODES)).reshape(8, 4)
    slab = np.arange(SLABS)
    cosine, sine = turn(z_freq[:, :, None], 8 * slab[None, None, :])
    cosine, sine = cosine[:, :, None, :], sine[:, :, None, :]
    forward_z = np.zeros((8, 4, 4, 2, 2, SLABS, 2, 4))
    for q in range(4):
        forward_z[:, q, :, :, 0, :, 0, q], forward_z[:, q, :, :, 0, :, 1, q] = cosine, sine
        forward_z[:, q, :, :, 1, :, 0, q], forward_z[:, q, :, :, 1, :, 1, q] = -sine, cosine
    forward_z = forward_z.reshape(MODE_ROWS, SLABS, 8)
    kinds = [forward_z]
    for order in ([3, 2, 1, 0], [0, 2, 1, 3]):
        mirrored = np.zeros_like(forward_z)
        for q in range(4):
            mirrored[:, :, order[q]] = forward_z[:, :, q]
            mirrored[:, :, 4 + order[q]] = -forward_z[:, :, 4 + q]
        kinds.append(mirrored)
    kinds = np.stack(kinds).reshape(3, MODE_ROWS, 256)
    made["zf"] = np.stack(pieces(kinds), axis=1)
    made["zi"] = np.stack(pieces(kinds.transpose(0, 2, 1)), axis=1)
    cosine, sine = turn(z_freq[:, :, None], np.arange(PLANES)[None, None, :])
    spread = np.zeros((2, 8, 4, 4, 2, 2, PLANES, CHAN))
    spread[0] = cosine[:, None, :, None, None, :, None]
    spread[1, :, :, :, :, 0] = sine[:, None, :, None, :, None]
    spread[1, :, :, :, :, 1] = -sine[:, None, :, None, :, None]
    made["tw"] = spread.reshape(2, MODE_ROWS // 8, 8, LANES).astype(np.float32)

    same = np.eye(CHAN)
    of_output = np.broadcast_to(same[None, :, :, None], (PLANES, CHAN, CHAN, CHAN)).reshape(LANES, 256)
    of_input = np.broadcast_to(same[None, :, None, :], (PLANES, CHAN, CHAN, CHAN)).reshape(LANES, 256)
    made["eo"] = (np.concatenate([of_output, of_output]) * float(GRID) ** -3).astype(ml_dtypes.bfloat16)
    made["ei"] = np.concatenate([of_input, of_input]).astype(ml_dtypes.bfloat16)
    made["es"] = np.concatenate([of_input.T[:LANES]] * 2).astype(ml_dtypes.bfloat16)
    return made


TABLE_NAMES = ("xf", "yf", "zf", "zi", "tw", "eo", "ei", "es", "yi", "ye", "xi")


def product(a, b):
    return lax.dot_general(a, b, (((1,), (0,)), ((), ())), preferred_element_type=F32)


def product_t(a, b):
    return lax.dot_general(a, b, (((1,), (1,)), ((), ())), preferred_element_type=F32)


def exact_product(a, b, dims):
    return lax.dot_general(a, b, (dims, ((), ())), precision=lax.Precision.HIGHEST, preferred_element_type=F32)


def split(value):
    high = value.astype(BF16)
    return high, (value - high.astype(F32)).astype(BF16)


def stacked(value):
    high, low = split(value)
    return jnp.concatenate([high, low, high], axis=0)


def gelu_slope(value):
    normal_cdf = 0.5 * (1.0 + lax.erf(value * 0.7071067811865476))
    density = jnp.exp(-0.5 * value * value) * 0.3989422804014327
    return normal_cdf + value * density


def parts_swapped(tile):
    even = lax.broadcasted_iota(jnp.int32, tile.shape, 1) % 2 == 0
    return jnp.where(even, pltpu.roll(tile, 7, 1), pltpu.roll(tile, 1, 1))


def to_pencil(src, dst, send, recv, d):
    return pltpu.make_async_remote_copy(
        src_ref=src,
        dst_ref=dst,
        send_sem=send,
        recv_sem=recv,
        device_id={"pencil": d},
        device_id_type=pl.DeviceIdType.MESH,
    )


def to_slab(src, dst, send, recv, d):
    return pltpu.make_async_remote_copy(
        src_ref=src,
        dst_ref=dst,
        send_sem=send,
        recv_sem=recv,
        device_id={"slab": d},
        device_id_type=pl.DeviceIdType.MESH,
    )


def first_tiles(x):
    return pl.ds(x * FIRST, FIRST)


def rest_tiles(x):
    return pl.ds(CHIPS * FIRST + x * REST, REST)


def y_index(p, q):
    if q < 2:
        return 2 * p + q
    if q == 2:
        return 31 - 2 * p
    return jnp.where(p == 0, 16, 32 - 2 * p)


def modes_kernel(
    act_hbm, pre_hbm, cot_hbm, weight_hbm, local_hbm,
    xf_hbm, yf_hbm, zf_hbm, zi_hbm, tw_hbm, eo_hbm, ei_hbm, es_hbm, yi_hbm, ye_hbm, xi_hbm,
    result_hbm, grad_hbm, sum_hbm,
    act, pre, cot, g_high, g_low, local_part, result,
    xf, yf, zf, zi, tw, eo, ei, es, yi, ye, xi,
    field_x, spread_y,
    out1, pair_in, sum1, in1, edge_in, out2, in2,
    weights, weight_parts, low_modes, out3, in3, out4, in4, edge4, grads,
    sums_acc, sums_a, sums_y, sums_z, sums_mine, sums_all, local_ref, mix,
    table_sem, load_sem, store_sem, own_sem,
    psend, precv, send1, recv1, esend, erecv, send2, recv2, wsend, wrecv,
    send3, recv3, send4, recv4, fsend, xsend, xrecv, gsend, grecv,
    asend, arecv, ysend, yrecv, zsend, zrecv,
):
    slab = lax.axis_index("slab")
    pencil = lax.axis_index("pencil")
    core, chip = pencil % CORES, pencil // CORES
    other = chip * CORES + 1 - core

    my_z, my_y = slab // 4, slab % 4

    slab_peers = [
        (slab // 4 + far_z) % 8 * 4 + (slab + far_y) % 4
        for far_z in (4, 3, 5, 2, 6, 1, 7, 0)
        for far_y in (2, 1, 3, 0)
        if far_z or far_y
    ]

    chunks = ROWS // CHUNK
    loads = []
    for c, (start, stop) in enumerate(LOADS):
        rows = pl.ds(start, stop - start)
        loads.append(
            [
                pltpu.make_async_copy(pre_hbm.at[rows], pre.at[rows], load_sem.at[0, c]),
                pltpu.make_async_copy(cot_hbm.at[rows], cot.at[rows], load_sem.at[1, c]),
                pltpu.make_async_copy(act_hbm.at[rows], act.at[rows], load_sem.at[2, c]),
            ]
        )
    kind = jnp.where(slab < 16, 0, jnp.where(pencil == 0, 2, 1))
    sources = (
        (xf_hbm, xf), (yf_hbm.at[pencil], yf), (zf_hbm.at[kind], zf), (zi_hbm.at[kind], zi), (tw_hbm, tw), (eo_hbm, eo), (ei_hbm, ei), (es_hbm, es),
        (yi_hbm.at[pencil], yi), (ye_hbm.at[pencil], ye), (xi_hbm, xi),
        (local_hbm, local_ref),
    )
    fetch = [pltpu.make_async_copy(a, b, table_sem.at[n]) for n, (a, b) in enumerate(sources)]
    by_name = dict(zip(TABLE_NAMES + ("local",), fetch))
    loads[0][0].start()
    loads[0][1].start()
    by_name["xf"].start()
    for load in loads[1:]:
        load[0].start()
        load[1].start()
    by_name["yf"].start()
    for load in loads:
        load[2].start()
    for name in by_name:
        if name not in ("xf", "yf"):
            by_name[name].start()

    barrier = pltpu.get_barrier_semaphore()

    @pl.loop(1, PENCILS)
    def _(j):
        pl.semaphore_signal(
            barrier, inc=1, device_id={"pencil": (pencil + j) % PENCILS}, device_id_type=pl.DeviceIdType.MESH
        )

    @pl.loop(1, SLABS)
    def _(j):
        pl.semaphore_signal(barrier, inc=1, device_id={"slab": (slab + j) % SLABS}, device_id_type=pl.DeviceIdType.MESH)

    def gradient_values(step):
        for r in range(PAIR):
            y = step * PAIR + r
            for part in range(4):
                rows = pl.ds(part * (LANES // 4), LANES // 4)
                g = cot[y, rows].astype(F32) * gelu_slope(pre[y, rows].astype(F32))
                high, low = split(g)
                g_high[y, rows] = high
                g_low[y, rows] = low

    def store_modes(t, step, modes):
        for r in range(PAIR):
            place = (step * PAIR + r) * XROWS
            place = place if isinstance(place, int) else pl.multiple_of(place, 8)
            field_x[t, pl.ds(place, XROWS), :] = modes[:, r * LANES : (r + 1) * LANES]

    def gradient_modes(step):
        rows = pl.ds(step * PAIR, PAIR)
        both = product_t(xf[...], g_high[rows].reshape(PAIR * LANES, GRID))
        more = product_t(xf[:XPAD], g_low[rows].reshape(PAIR * LANES, GRID))
        store_modes(0, step, both[:XROWS] + both[XPAD : XPAD + XROWS] + more[:XROWS])

    for c, (start, stop) in enumerate(LOADS):
        loads[c][0].wait()
        loads[c][1].wait()
        if c == 0:
            by_name["xf"].wait()
            gradient_values(0)

        for step in range(max(start // PAIR, 1), stop // PAIR):
            gradient_modes(step - 1)
            gradient_values(step)

    gradient_modes(ROWS // PAIR - 1)

    def send_rows(t):
        out1[t, 0, BLOCK - 1] = jnp.zeros((8, LANES), F32)
        out1[t, 1, EDGE:BLOCK] = jnp.zeros((BLOCK - EDGE, 8, LANES), F32)
        for half, ks in enumerate((range(FIRST), range(FIRST, HALF))):
            for first in range(ks.start, ks.stop, 2):
                group = range(first, min(first + 2, ks.stop))
                columns = []
                for k in group:
                    real = field_x[t, pl.ds(k, ROWS, stride=XROWS), :]
                    imag = field_x[t, pl.ds(HALF + k, ROWS, stride=XROWS), :]
                    columns.append(jnp.concatenate([real, imag], axis=0))
                both = product(yf[...], stacked(jnp.concatenate(columns, axis=1)))
                for k in group:
                    modes = both[:, (k - first) * LANES : (k - first + 1) * LANES]
                    for d in range(PENCILS):
                        x = d // CORES
                        place = x * FIRST + k if k < FIRST else CHIPS * FIRST + x * REST + k - FIRST
                        out1[t, d % CORES, place] = modes[8 * d : 8 * d + 8]
                    out1[t, 0, EDGE + k // 4, 2 * (k % 4) : 2 * (k % 4) + 2] = modes[64:66]
            pair_copy(t, half).start()

    def pair_copy(t, half):
        tiles = pl.ds(0, CHIPS * FIRST) if half == 0 else pl.ds(CHIPS * FIRST, BLOCK - CHIPS * FIRST)
        return to_pencil(
            out1.at[t, 1 - core, tiles], pair_in.at[t, tiles], psend.at[t], precv.at[t, half], other
        )

    halves = (first_tiles, rest_tiles)
    spans = (pl.ds(0, FIRST), pl.ds(FIRST, REST))

    def x_copy(t, half, to, source):
        return to_pencil(
            sum1.at[t, halves[half](to)], in1.at[t, source, spans[half]], send1.at[t, half], recv1.at[t, source, half],
            to * CORES + core,
        )

    def send_sums(t):
        for half in range(2):
            pair_copy(t, half).wait_recv()
            for j in (2, 1, 3, 0):
                x = (chip + j) % CHIPS
                tiles = halves[half](x)
                sum1[t, tiles] = out1[t, core, tiles] + pair_in[t, tiles]
                if j:
                    x_copy(t, half, x, chip).start()
        sum1[t, EDGE:BLOCK] = out1[t, core, EDGE:BLOCK] + pair_in[t, EDGE:BLOCK]

        @pl.when((core == 0) & (chip != 0))
        def _():
            to_pencil(
                sum1.at[t, pl.ds(EDGE, BLOCK - EDGE)], edge_in.at[t, chip], esend.at[t], erecv.at[t, chip], 0
            ).start()

    by_name["yf"].wait()
    pl.semaphore_wait(barrier, PENCILS - 1 + SLABS - 1)
    send_rows(0)
    send_sums(0)

    @pl.loop(1, PENCILS)
    def _(j):
        d = (pencil + j) % PENCILS
        to_pencil(weight_hbm.at[pl.ds(2 * d, 2)], weights.at[pl.ds(4 * pencil, 2)], wsend, wrecv, d).start()

        @pl.when(d != 0)
        def _():
            to_pencil(
                weight_hbm.at[pl.ds(31 - 2 * d, 2)], weights.at[pl.ds(4 * pencil + 2, 2)], wsend, wrecv, d
            ).start()

        @pl.when(d == 0)
        def _():
            to_pencil(weight_hbm.at[31], weights.at[4 * pencil + 2], wsend, wrecv, d).start()
            to_pencil(weight_hbm.at[16], weights.at[4 * pencil + 3], wsend, wrecv, d).start()

    for q in range(4):
        pltpu.make_async_copy(weight_hbm.at[y_index(pencil, q)], weights.at[4 * pencil + q], own_sem.at[q]).start()

    for c, (start, stop) in enumerate(LOADS):
        loads[c][2].wait()

        @pl.loop(start // PAIR, stop // PAIR, unroll=True)
        def _(step):
            both = product_t(xf[...], act[pl.ds(step * PAIR, PAIR)].reshape(PAIR * LANES, GRID))
            store_modes(1, step, both[:XROWS] + both[XPAD : XPAD + XROWS])

    send_rows(1)
    lane = lax.broadcasted_iota(jnp.int32, (LANES, LANES), 1) // CHAN
    row = lax.broadcasted_iota(jnp.int32, (LANES, LANES), 0) // CHAN

    def send_tiles(t):
        for half, ks in enumerate((range(FIRST), range(FIRST, HALF))):
            total = sum1[t, halves[half](chip)]
            for j in range(1, CHIPS):
                x = (chip + j) % CHIPS
                x_copy(t, half, x, x).wait_recv()
                total = total + in1[t, x, spans[half]]
            for k in ks:
                if k < 16:
                    out2[t, k] = total[k - ks.start]
                if k > 0:
                    out2[t, MODES - k] = total[k - ks.start]

        @pl.when(pencil == 0)
        def _():
            edge = sum1[t, EDGE:BLOCK]
            for x in range(1, CHIPS):
                to_pencil(
                    sum1.at[t, pl.ds(EDGE, BLOCK - EDGE)], edge_in.at[t, x], esend.at[t], erecv.at[t, x], 0
                ).wait_recv()
                edge = edge + edge_in[t, x]
            for k in range(1, HALF):
                r = 2 * (k % 4)
                out2[t, MODES - k, 3:4] = edge[k // 4, r : r + 1]
                out2[t, MODES - k, 7:8] = edge[k // 4, r + 1 : r + 2]

        for d in slab_peers:
            to_slab(out2.at[t, d], in2.at[t, slab], send2.at[t], recv2.at[t], d).start()

        in2[t, slab] = out2[t, slab]

    send_tiles(0)
    send_sums(1)

    sums_acc[...] = jnp.zeros_like(sums_acc)

    @pl.loop(0, ROWS, step=4, unroll=True)
    def _(first):
        left, right = [], []
        for r in range(4):
            left.append(jnp.concatenate([g_high[first + r], g_low[first + r]], axis=0))
            right.append(act[first + r])
        sums_acc[...] += product_t(jnp.concatenate(left, axis=1), jnp.concatenate(right, axis=1))

    full = jnp.where(lane == row, sums_acc[:LANES] + sums_acc[LANES:], 0.0)
    full = jnp.sum(full.reshape(PLANES, CHAN, LANES), axis=0)
    for shift in (CHAN, 2 * CHAN, 4 * CHAN):
        full = full + pltpu.roll(full, shift, 1)
    o_row = lax.broadcasted_iota(jnp.int32, (CHAN, LANES), 0) % 8
    o_lane = lax.broadcasted_iota(jnp.int32, (CHAN, LANES), 1) // CHAN
    full = jnp.where(o_row == o_lane, full, 0.0).reshape(2, 8, LANES)
    full = jnp.sum(full, axis=1, keepdims=True)
    place = lax.broadcasted_iota(jnp.int32, (8, LANES), 0)
    sums_mine[...] = jnp.where(place == 0, full[0], jnp.where(place == 1, full[1], 0.0))

    @pl.loop(1, PENCILS)
    def _(j):
        d = (pencil + j) % PENCILS
        to_pencil(sums_mine, sums_a.at[pencil], asend, arecv.at[pencil], d).start()

    for name in TABLE_NAMES[2:]:
        by_name[name].wait()

    mode_tiles = (MODE_ROWS // 8, 8, LANES)
    place = lax.broadcasted_iota(jnp.int32, mode_tiles, 1)
    first_part = place % 2 == 0
    first_half = place % 4 < 2

    def z_product(table, value):
        high, low = split(value)
        both = product(table[0], jnp.concatenate([high, low], axis=1))
        return both[:, :LANES] + both[:, LANES:] + product(table[1], high)

    def modes_of(t, expand):
        most = pl.ds(0, SLABS - 1)
        to_slab(out2.at[t, most], in2.at[t, most], send2.at[t], recv2.at[t], slab).wait_recv()
        found = z_product(zf, in2[t].reshape(256, LANES)).reshape(mode_tiles)
        found = found * tw[0] + parts_swapped(found) * tw[1]
        high, low = split(found.reshape(MODE_ROWS, LANES))
        wide = product(jnp.concatenate([high, low], axis=1), expand)
        return jnp.where(first_half, wide[:, :LANES].reshape(mode_tiles), wide[:, LANES:].reshape(mode_tiles))

    def both_parts(tile):
        swapped = parts_swapped(tile)
        return jnp.where(first_part, tile, swapped), jnp.where(first_part, swapped, tile)

    to_pencil(
        weight_hbm.at[pl.ds(0, 28)], weights.at[pl.ds(0, 28)], wsend, wrecv, pencil
    ).wait_recv()
    for q in range(4):
        pltpu.make_async_copy(weight_hbm.at[y_index(pencil, q)], weights.at[4 * pencil + q], own_sem.at[q]).wait()
    weight_parts[0], weight_parts[1] = both_parts(weights[...].reshape(mode_tiles))

    lower = modes_of(0, eo[...])
    swapped = parts_swapped(lower)
    turned = jnp.where(first_part, swapped, -swapped)
    low_modes[0] = lower
    low_modes[1] = turned
    high, low = split((weight_parts[0] * lower + weight_parts[1] * turned).reshape(MODE_ROWS, LANES))
    back = product(jnp.concatenate([high, low], axis=1), es[...]).reshape(mode_tiles)
    back = back * tw[0] - parts_swapped(back) * tw[1]
    out3[...] = z_product(zi, back.reshape(MODE_ROWS, LANES)).reshape(SLABS, 8, LANES)

    for d in slab_peers:
        to_slab(out3.at[d], in3.at[slab], send3, recv3, d).start()

    in3[slab] = out3[slab]

    pick = jnp.where(
        lax.broadcasted_iota(jnp.int32, (LANES, CHAN), 0) % CHAN == lax.broadcasted_iota(jnp.int32, (LANES, CHAN), 1),
        1.0,
        0.0,
    )
    by_name["local"].wait()
    mixed = exact_product(pick, local_ref[...], ((1,), (1,)))
    mixed = exact_product(mixed, pick, ((1,), (1,)))
    mix_high, mix_low = split(jnp.where(lane == row, mixed, 0.0))
    mix_rows = jnp.concatenate([mix_high, mix_high], axis=1)
    mix_more = jnp.concatenate([mix_low, jnp.zeros_like(mix_low)], axis=1)
    mix[...] = jnp.concatenate([mix_rows, mix_more], axis=0)

    @pl.loop(0, ROWS, unroll=4)
    def _(y):
        both = product(mix[...], jnp.concatenate([g_high[y], g_low[y]], axis=0))
        local_part[y] = both[:LANES] + both[LANES:]


    sums_a[pencil] = sums_mine[...]
    for j in range(1, PENCILS):
        d = (pencil + j) % PENCILS
        to_pencil(sums_mine, sums_a.at[d], asend, arecv.at[d], d).wait_recv()
    total = jnp.zeros((8, LANES), F32)
    for d in range(PENCILS):
        total = total + sums_a[d]
    sums_y[my_y] = total
    for j in range(1, 4):
        to_slab(sums_y.at[my_y], sums_y.at[my_y], ysend, yrecv, my_z * 4 + (my_y + j) % 4).start()

    send_tiles(1)

    def back_copy(half, p, to, sem):
        return to_pencil(out4.at[spans[half]], in4.at[p, spans[half]], sem, recv4.at[p, half], to)

    to_slab(out3.at[pl.ds(0, SLABS - 1)], in3.at[pl.ds(0, SLABS - 1)], send3, recv3, slab).wait_recv()
    for half, ks in enumerate((range(FIRST), range(FIRST, HALF))):
        for k in ks:
            out4[k] = in3[k] + in3[MODES - k] if 0 < k < 16 else in3[k]

        @pl.when(pencil == 0)
        def _():
            for k in ks:
                for part in range(2):
                    r = 3 + 4 * part
                    if k > 0:
                        edge4[2 * k + part : 2 * k + part + 1] = in3[MODES - k, r : r + 1]
                        out4[k, r : r + 1] = in3[k, r : r + 1] if k < 16 else jnp.zeros((1, LANES), F32)

        for j in (2, 1, 3):
            x = (chip + j) % CHIPS
            back_copy(half, pencil, x * CORES + core, send4.at[half]).start()
        back_copy(half, pencil, other, send4.at[2]).start()

    @pl.when(pencil == 0)
    def _():
        edge4[0:2] = jnp.zeros((2, LANES), F32)
        edge4[34:40] = jnp.zeros((6, LANES), F32)

        @pl.loop(1, PENCILS)
        def _(d):
            to_pencil(edge4, edge4, xsend, xrecv, d).start()

    in4[pencil] = out4[...]

    upper = modes_of(1, ei[...])
    real, imag = both_parts(upper)
    grads[...] = (low_modes[0] * real + low_modes[1] * imag).reshape(MODES, 16, LANES)

    @pl.loop(1, PENCILS)
    def _(j):
        d = (pencil + j) % PENCILS
        to_pencil(grads.at[pl.ds(4 * d, 2)], grad_hbm.at[pl.ds(2 * pencil, 2)], gsend, grecv, d).start()

        @pl.when(pencil != 0)
        def _():
            to_pencil(
                grads.at[pl.ds(4 * d + 2, 2)], grad_hbm.at[pl.ds(31 - 2 * pencil, 2)], gsend, grecv, d
            ).start()

        @pl.when(pencil == 0)
        def _():
            to_pencil(grads.at[4 * d + 2], grad_hbm.at[31], gsend, grecv, d).start()
            to_pencil(grads.at[4 * d + 3], grad_hbm.at[16], gsend, grecv, d).start()

    for q in range(4):
        pltpu.make_async_copy(grads.at[4 * pencil + q], grad_hbm.at[y_index(pencil, q)], own_sem.at[4 + q]).start()

    to_slab(sums_y.at[pl.ds(0, 3)], sums_y.at[pl.ds(0, 3)], ysend, yrecv, slab).wait_recv()
    total = sums_y[0]
    for j in range(1, 4):
        total = total + sums_y[j]
    sums_z[my_z] = total
    for j in range(1, 8):
        to_slab(sums_z.at[my_z], sums_z.at[my_z], zsend, zrecv, (my_z + j) % 8 * 4 + my_y).start()

    for half in range(2):
        for j in (1, 3, 2):
            d = (chip + j) % CHIPS * CORES + core
            back_copy(half, d, d, send4.at[half]).wait_recv()
            to_pencil(
                in4.at[d, spans[half]], in4.at[d, spans[half]], fsend.at[half], recv4.at[d, half], other
            ).start()

    @pl.when(pencil != 0)
    def _():
        to_pencil(edge4, edge4, xsend, xrecv, 0).wait_recv()

    spread_y[pl.ds(2 * HALF * ROWS, (XROWS - 2 * HALF) * ROWS), :] = jnp.zeros(((XROWS - 2 * HALF) * ROWS, LANES), F32)
    for half, ks in enumerate((range(FIRST), range(FIRST, HALF))):
        for x in range(CHIPS):
            back_copy(half, x * CORES + 1 - core, other, send4.at[2]).wait_recv()
        for first in range(ks.start, ks.stop, 2):
            group = range(first, min(first + 2, ks.stop))
            columns = [jnp.concatenate([in4[p, k] for p in range(PENCILS)], axis=0) for k in group]
            both = product(yi[...], stacked(jnp.concatenate(columns, axis=1)))
            for k in group:
                field = both[:, (k - first) * LANES : (k - first + 1) * LANES]
                edge_real, edge_imag = edge4[2 * k : 2 * k + 1], edge4[2 * k + 1 : 2 * k + 2]
                spread_y[k * ROWS : (k + 1) * ROWS] = field[:ROWS] + ye[0] * edge_real - ye[1] * edge_imag
                spread_y[(HALF + k) * ROWS : (HALF + k + 1) * ROWS] = (
                    field[ROWS:] + ye[0] * edge_imag + ye[1] * edge_real
                )

    to_slab(sums_z.at[pl.ds(0, 7)], sums_z.at[pl.ds(0, 7)], zsend, zrecv, slab).wait_recv()
    total = sums_z[0]
    for j in range(1, 8):
        total = total + sums_z[j]
    sums_all[...] = total * float(GRID) ** -1.5
    stores = [pltpu.make_async_copy(sums_all, sum_hbm, store_sem.at[chunks])]
    stores[0].start()

    for c in range(chunks):

        columns = []
        for r in range(CHUNK):
            value = spread_y[pl.ds(c * CHUNK + r, XROWS, stride=ROWS), :]
            high = value.astype(BF16).astype(F32)
            column = jnp.concatenate([high, value - high, high, jnp.zeros((8, LANES), F32)], axis=0)
            columns.append(column.T.astype(BF16))
        fields = product(jnp.concatenate(columns, axis=0), xi[...])
        for r in range(CHUNK):
            y = c * CHUNK + r
            result[y] = (local_part[y] + fields[r * LANES : (r + 1) * LANES]).astype(BF16)

        rows = pl.ds(c * CHUNK, CHUNK)
        stores.append(pltpu.make_async_copy(result.at[rows], result_hbm.at[rows], store_sem.at[c]))
        stores[-1].start()

    to_pencil(weights.at[pl.ds(0, 28)], weights.at[pl.ds(0, 28)], wsend, wrecv, pencil).wait_send()
    for t in range(2):
        to_pencil(out1.at[t, 1 - core], pair_in.at[t], psend.at[t], precv.at[t, 0], other).wait_send()
        for half in range(2):
            some = in1.at[t, pl.ds(0, 3), spans[half]]
            to_pencil(some, some, send1.at[t, half], recv1.at[t, 0, half], other).wait_send()
        most = pl.ds(0, SLABS - 1)
        to_slab(out2.at[t, most], in2.at[t, most], send2.at[t], recv2.at[t], slab).wait_send()

        @pl.when((core == 0) & (chip != 0))
        def _():
            to_pencil(
                sum1.at[t, pl.ds(EDGE, BLOCK - EDGE)], edge_in.at[t, chip], esend.at[t], erecv.at[t, chip], 0
            ).wait_send()

    to_pencil(sums_a.at[pl.ds(0, 7)], sums_a.at[pl.ds(0, 7)], asend, arecv.at[0], pencil).wait_send()
    to_slab(sums_y.at[pl.ds(0, 3)], sums_y.at[pl.ds(0, 3)], ysend, yrecv, slab).wait_send()
    to_slab(sums_z.at[pl.ds(0, 7)], sums_z.at[pl.ds(0, 7)], zsend, zrecv, slab).wait_send()
    to_slab(out3.at[pl.ds(0, 31)], in3.at[pl.ds(0, 31)], send3, recv3, slab).wait_send()
    for half in range(2):
        some = in4.at[pl.ds(0, 3), spans[half]]
        to_pencil(some, some, send4.at[half], recv4.at[0, half], other).wait_send()
        to_pencil(some, some, fsend.at[half], recv4.at[0, half], other).wait_send()
    to_pencil(out4, in4.at[pencil], send4.at[2], recv4.at[pencil, 0], other).wait_send()

    @pl.when(pencil == 0)
    def _():
        for d in range(1, PENCILS):
            to_pencil(edge4, edge4, xsend, xrecv, d).wait_send()

    to_pencil(grads.at[pl.ds(0, 28)], grad_hbm.at[pl.ds(0, 28)], gsend, grecv, pencil).wait()
    for q in range(4):
        pltpu.make_async_copy(grads.at[4 * pencil + q], grad_hbm.at[y_index(pencil, q)], own_sem.at[4 + q]).wait()
    for store in stores:
        store.wait()


def last_kernel(
    result_hbm, grad_in, sum_hbm,
    out_hbm, local_hbm, grad_out,
    result, grad, sum_ref, local_ref, load_sem, store_sem,
):
    rows = [pl.ds(c * (ROWS // PARTS), ROWS // PARTS) for c in range(PARTS)]
    loads = [pltpu.make_async_copy(result_hbm.at[r], result.at[r], load_sem.at[c]) for c, r in enumerate(rows)]
    stores = [pltpu.make_async_copy(result.at[r], out_hbm.at[r], store_sem.at[c]) for c, r in enumerate(rows)]
    loads.append(pltpu.make_async_copy(grad_in, grad, load_sem.at[PARTS]))
    stores.append(pltpu.make_async_copy(grad, grad_out, store_sem.at[PARTS]))
    load_sum = pltpu.make_async_copy(sum_hbm, sum_ref, load_sem.at[PARTS + 1])
    load_sum.start()
    for load in loads:
        load.start()

    o_row = lax.broadcasted_iota(jnp.int32, (CHAN, LANES), 0)
    o_lane = lax.broadcasted_iota(jnp.int32, (CHAN, LANES), 1)
    load_sum.wait()
    total = jnp.where(o_row < 8, sum_ref[0:1], sum_ref[1:2])
    total = jnp.where(o_row % 8 == o_lane // CHAN, total, 0.0)
    pick = jnp.where(
        lax.broadcasted_iota(jnp.int32, (LANES, CHAN), 0) % CHAN == lax.broadcasted_iota(jnp.int32, (LANES, CHAN), 1),
        1.0,
        0.0,
    )
    local_ref[...] = exact_product(total, pick, ((1,), (0,)))
    store_local = pltpu.make_async_copy(local_ref, local_hbm, store_sem.at[PARTS + 1])
    store_local.start()
    for load, store in zip(loads, stores):
        load.wait()
        store.start()
    for store in stores:
        store.wait()
    store_local.wait()


def on_device(activation, preact, cotangent, local_weight, spectral_weight):
    made = tables()
    fields = [a.reshape(ROWS, LANES, GRID) for a in (activation, preact, cotangent)]
    weight = spectral_weight[0].reshape(MODES, 4, 2, 2, LANES).transpose(0, 1, 3, 2, 4).reshape(MODES, 16, LANES)
    any_space = pl.BlockSpec(memory_space=pl.ANY)
    dma = pltpu.SemaphoreType.DMA
    field = pltpu.VMEM((ROWS, LANES, GRID), BF16)
    wide_field = pltpu.VMEM((ROWS, LANES, GRID), F32)
    tile = (8, LANES)
    result, grad, total = pl.pallas_call(
        modes_kernel,
        out_shape=(
            jax.ShapeDtypeStruct((ROWS, LANES, GRID), BF16),
            jax.ShapeDtypeStruct((MODES, 16, LANES), F32),
            jax.ShapeDtypeStruct(tile, F32),
        ),
        in_specs=[any_space] * (5 + len(TABLE_NAMES)),
        out_specs=(any_space, any_space, any_space),
        scratch_shapes=[
            field, field, field, field, field, wide_field, field,
            pltpu.VMEM((2 * XPAD, GRID), BF16),
            pltpu.VMEM((80, 192), BF16),
            pltpu.VMEM((2, MODE_ROWS, 256), BF16),
            pltpu.VMEM((2, 256, MODE_ROWS), BF16),
            pltpu.VMEM((2, MODE_ROWS // 8, 8, LANES), F32),
            pltpu.VMEM((256, 256), BF16),
            pltpu.VMEM((256, 256), BF16),
            pltpu.VMEM((256, LANES), BF16),
            pltpu.VMEM((64, 192), BF16),
            pltpu.VMEM((2, ROWS, LANES), F32),
            pltpu.VMEM((128, GRID), BF16),
            pltpu.VMEM((2, ROWS * XROWS, LANES), F32),
            pltpu.VMEM((ROWS * XROWS, LANES), F32),
            pltpu.VMEM((2, CORES, BLOCK) + tile, F32),
            pltpu.VMEM((2, BLOCK) + tile, F32),
            pltpu.VMEM((2, BLOCK) + tile, F32),
            pltpu.VMEM((2, CHIPS, HALF) + tile, F32),
            pltpu.VMEM((2, CHIPS, BLOCK - EDGE) + tile, F32),
            pltpu.VMEM((2, SLABS) + tile, F32),
            pltpu.VMEM((2, SLABS) + tile, F32),
            pltpu.VMEM((MODES, 16, LANES), F32),
            pltpu.VMEM((2, MODE_ROWS // 8, 8, LANES), F32),
            pltpu.VMEM((2, MODE_ROWS // 8, 8, LANES), F32),
            pltpu.VMEM((SLABS,) + tile, F32),
            pltpu.VMEM((SLABS,) + tile, F32),
            pltpu.VMEM((HALF,) + tile, F32),
            pltpu.VMEM((PENCILS, HALF) + tile, F32),
            pltpu.VMEM((XROWS, LANES), F32),
            pltpu.VMEM((MODES, 16, LANES), F32),
            pltpu.VMEM((2 * LANES, LANES), F32),
            pltpu.VMEM((PENCILS,) + tile, F32),
            pltpu.VMEM((4,) + tile, F32),
            pltpu.VMEM((8,) + tile, F32),
            pltpu.VMEM(tile, F32),
            pltpu.VMEM(tile, F32),
            pltpu.VMEM((CHAN, CHAN), F32),
            pltpu.VMEM((2 * LANES, 2 * LANES), BF16),
            dma((len(TABLE_NAMES) + 1,)), dma((3, len(LOADS))), dma((ROWS // CHUNK + 1,)), dma((8,)),
            dma((2,)), dma((2, 2)), dma((2, 2)), dma((2, CHIPS, 2)), dma((2,)), dma((2, CHIPS)),
            dma((2,)), dma((2,)), dma, dma,
            dma, dma, dma((3,)), dma((PENCILS, 2)), dma((2,)), dma, dma, dma, dma,
            dma, dma((PENCILS,)), dma, dma, dma, dma,
        ],
        compiler_params=pltpu.CompilerParams(
            collective_id=0, has_side_effects=True, vmem_limit_bytes=62 * 1024 * 1024
        ),
        cost_estimate=pl.CostEstimate(flops=3_000_000_000, bytes_accessed=11_000_000, transcendentals=2_000_000),
        name="modes",
    )(*fields, weight, local_weight, *(jnp.asarray(made[name]) for name in TABLE_NAMES))
    out, grad_local, grad_spectral = pl.pallas_call(
        last_kernel,
        out_shape=(
            jax.ShapeDtypeStruct((ROWS, LANES, GRID), BF16),
            jax.ShapeDtypeStruct((CHAN, CHAN), F32),
            jax.ShapeDtypeStruct((MODES, 16, LANES), F32),
        ),
        in_specs=[any_space, any_space, any_space],
        out_specs=(any_space, any_space, any_space),
        scratch_shapes=[
            field,
            pltpu.VMEM((MODES, 16, LANES), F32),
            pltpu.VMEM(tile, F32),
            pltpu.VMEM((CHAN, CHAN), F32),
            dma((PARTS + 2,)), dma((PARTS + 2,)),
        ],
        compiler_params=pltpu.CompilerParams(vmem_limit_bytes=62 * 1024 * 1024),
        cost_estimate=pl.CostEstimate(flops=100_000, bytes_accessed=5_000_000, transcendentals=0),
        name="last",
    )(result, grad, total)
    grad_spectral = grad_spectral.reshape(MODES, 4, 2, 2, LANES).transpose(0, 1, 3, 2, 4).reshape(spectral_weight.shape)
    return out.reshape(activation.shape), grad_local, grad_spectral


def solution(mesh):
    field = P("pencil", "slab", None, None)
    modes = P("slab", None, "pencil", None, None)
    return jax.shard_map(
        on_device,
        mesh=mesh,
        in_specs=(field, field, field, P(), modes),
        out_specs=(field, P(), modes),
        check_vma=False,
    )
```

```python
import functools

import jax
import jax.numpy as jnp
import ml_dtypes
import numpy as np
from jax import lax
from jax.experimental import pallas as pl
from jax.experimental.pallas import tpu as pltpu
from jax.sharding import PartitionSpec as P

GRID = 256
CHAN = 16
MODES = 32
SLABS = 32
PENCILS = 8
ROWS = GRID // PENCILS
PLANES = GRID // SLABS
LANES = PLANES * CHAN
HALF = MODES // 2 + 1
XROWS = 40
XPAD = 48
CORES = 2
CHIPS = PENCILS // CORES
FIRST = 9
REST = HALF - FIRST
EDGE = CHIPS * HALF
BLOCK = EDGE + XROWS // 8
PARTS = 8
MODE_ROWS = 512
CHUNK = 8
LOADS = ((0, 4), (4, 8), (8, 16), (16, 24), (24, 32))
PAIR = 2
F32 = jnp.float32
BF16 = jnp.bfloat16


def kept(j):
    return np.where(j < MODES // 2, j, j - MODES)


def y_set(p):
    if p == 0:
        return np.array([0, 1, -1, -16])
    return np.array([2 * p, 2 * p + 1, -2 * p - 1, -2 * p])


def pieces(table):
    high = table.astype(np.float32).astype(ml_dtypes.bfloat16)
    low = (table - high.astype(np.float64)).astype(np.float32).astype(ml_dtypes.bfloat16)
    return high, low


def turn(freq, position):
    angle = 2.0 * np.pi * ((freq * position) % GRID) / GRID
    return np.cos(angle), np.sin(angle)


@functools.cache
def tables():
    made = {}
    cells = np.arange(GRID)

    cosine, sine = turn(np.arange(HALF)[:, None], cells[None, :])
    forward_x = np.zeros((XPAD, GRID))
    forward_x[:HALF], forward_x[HALF : 2 * HALF] = cosine, -sine
    made["xf"] = np.concatenate(pieces(forward_x), axis=0)
    high, low = pieces(forward_x[:XROWS])
    made["xi"] = np.concatenate([high, high, low, np.zeros((8, GRID), high.dtype)], axis=0)

    forward_y = np.zeros((PENCILS, 80, 2, ROWS))
    inverse_y = np.zeros((PENCILS, 2, ROWS, PENCILS, 2, 4))
    extra_y = np.zeros((PENCILS, 2, ROWS, LANES))
    for p in range(PENCILS):
        rows = p * ROWS + np.arange(ROWS)
        for d in range(PENCILS):
            cosine, sine = turn(y_set(d)[:, None], rows[None, :])
            forward_y[p, 8 * d : 8 * d + 4, 0], forward_y[p, 8 * d : 8 * d + 4, 1] = cosine, sine
            forward_y[p, 8 * d + 4 : 8 * d + 8, 0], forward_y[p, 8 * d + 4 : 8 * d + 8, 1] = -sine, cosine
            inverse_y[p, 0, :, d, 0], inverse_y[p, 0, :, d, 1] = cosine.T, -sine.T
            inverse_y[p, 1, :, d, 0], inverse_y[p, 1, :, d, 1] = sine.T, cosine.T
        cosine, sine = turn(16, rows)
        forward_y[p, 64, 0], forward_y[p, 64, 1] = cosine, sine
        forward_y[p, 65, 0], forward_y[p, 65, 1] = -sine, cosine
        extra_y[p, 0], extra_y[p, 1] = cosine[:, None], sine[:, None]
    high, low = pieces(forward_y.reshape(PENCILS, 80, 2 * ROWS))
    made["yf"] = np.concatenate([high, high, low], axis=2)
    high, low = pieces(inverse_y.reshape(PENCILS, 2 * ROWS, 64))
    made["yi"] = np.concatenate([high, high, low], axis=2)
    made["ye"] = extra_y.astype(np.float32)

    z_freq = kept(np.arange(MODES)).reshape(8, 4)
    slab = np.arange(SLABS)
    cosine, sine = turn(z_freq[:, :, None], 8 * slab[None, None, :])
    cosine, sine = cosine[:, :, None, :], sine[:, :, None, :]
    forward_z = np.zeros((8, 4, 4, 2, 2, SLABS, 2, 4))
    for q in range(4):
        forward_z[:, q, :, :, 0, :, 0, q], forward_z[:, q, :, :, 0, :, 1, q] = cosine, sine
        forward_z[:, q, :, :, 1, :, 0, q], forward_z[:, q, :, :, 1, :, 1, q] = -sine, cosine
    forward_z = forward_z.reshape(MODE_ROWS, SLABS, 8)
    kinds = [forward_z]
    for order in ([3, 2, 1, 0], [0, 2, 1, 3]):
        mirrored = np.zeros_like(forward_z)
        for q in range(4):
            mirrored[:, :, order[q]] = forward_z[:, :, q]
            mirrored[:, :, 4 + order[q]] = -forward_z[:, :, 4 + q]
        kinds.append(mirrored)
    kinds = np.stack(kinds).reshape(3, MODE_ROWS, 256)
    made["zf"] = np.stack(pieces(kinds), axis=1)
    made["zi"] = np.stack(pieces(kinds.transpose(0, 2, 1)), axis=1)
    cosine, sine = turn(z_freq[:, :, None], np.arange(PLANES)[None, None, :])
    spread = np.zeros((2, 8, 4, 4, 2, 2, PLANES, CHAN))
    spread[0] = cosine[:, None, :, None, None, :, None]
    spread[1, :, :, :, :, 0] = sine[:, None, :, None, :, None]
    spread[1, :, :, :, :, 1] = -sine[:, None, :, None, :, None]
    made["tw"] = spread.reshape(2, MODE_ROWS // 8, 8, LANES).astype(np.float32)

    same = np.eye(CHAN)
    of_output = np.broadcast_to(same[None, :, :, None], (PLANES, CHAN, CHAN, CHAN)).reshape(LANES, 256)
    of_input = np.broadcast_to(same[None, :, None, :], (PLANES, CHAN, CHAN, CHAN)).reshape(LANES, 256)
    made["eo"] = (np.concatenate([of_output, of_output]) * float(GRID) ** -3).astype(ml_dtypes.bfloat16)
    made["ei"] = np.concatenate([of_input, of_input]).astype(ml_dtypes.bfloat16)
    made["es"] = np.concatenate([of_input.T[:LANES]] * 2).astype(ml_dtypes.bfloat16)
    return made


TABLE_NAMES = ("xf", "yf", "zf", "zi", "tw", "eo", "ei", "es", "yi", "ye", "xi")


def product(a, b):
    return lax.dot_general(a, b, (((1,), (0,)), ((), ())), preferred_element_type=F32)


def product_t(a, b):
    return lax.dot_general(a, b, (((1,), (1,)), ((), ())), preferred_element_type=F32)


def exact_product(a, b, dims):
    return lax.dot_general(a, b, (dims, ((), ())), precision=lax.Precision.HIGHEST, preferred_element_type=F32)


def split(value):
    high = value.astype(BF16)
    return high, (value - high.astype(F32)).astype(BF16)


def stacked(value):
    high, low = split(value)
    return jnp.concatenate([high, low, high], axis=0)


def gelu_slope(value):
    normal_cdf = 0.5 * (1.0 + lax.erf(value * 0.7071067811865476))
    density = jnp.exp(-0.5 * value * value) * 0.3989422804014327
    return normal_cdf + value * density


def parts_swapped(tile):
    even = lax.broadcasted_iota(jnp.int32, tile.shape, 1) % 2 == 0
    return jnp.where(even, pltpu.roll(tile, 7, 1), pltpu.roll(tile, 1, 1))


def to_pencil(src, dst, send, recv, d):
    return pltpu.make_async_remote_copy(
        src_ref=src,
        dst_ref=dst,
        send_sem=send,
        recv_sem=recv,
        device_id={"pencil": d},
        device_id_type=pl.DeviceIdType.MESH,
    )


def to_slab(src, dst, send, recv, d):
    return pltpu.make_async_remote_copy(
        src_ref=src,
        dst_ref=dst,
        send_sem=send,
        recv_sem=recv,
        device_id={"slab": d},
        device_id_type=pl.DeviceIdType.MESH,
    )


def first_tiles(x):
    return pl.ds(x * FIRST, FIRST)


def rest_tiles(x):
    return pl.ds(CHIPS * FIRST + x * REST, REST)


def y_index(p, q):
    if q < 2:
        return 2 * p + q
    if q == 2:
        return 31 - 2 * p
    return jnp.where(p == 0, 16, 32 - 2 * p)


def modes_kernel(
    act_hbm, pre_hbm, cot_hbm, weight_hbm, local_hbm,
    xf_hbm, yf_hbm, zf_hbm, zi_hbm, tw_hbm, eo_hbm, ei_hbm, es_hbm, yi_hbm, ye_hbm, xi_hbm,
    result_hbm, grad_hbm, sum_hbm,
    act, pre, cot, g_high, g_low, local_part, result,
    xf, yf, zf, zi, tw, eo, ei, es, yi, ye, xi,
    field_x, spread_y,
    out1, pair_in, sum1, in1, edge_in, out2, in2,
    weights, weight_parts, low_modes, out3, in3, out4, in4, edge4, grads,
    sums_acc, sums_a, sums_y, sums_z, sums_mine, sums_all, local_ref, mix,
    table_sem, load_sem, store_sem, own_sem,
    psend, precv, send1, recv1, esend, erecv, send2, recv2, wsend, wrecv,
    send3, recv3, send4, recv4, fsend, xsend, xrecv, gsend, grecv,
    asend, arecv, ysend, yrecv, zsend, zrecv,
):
    slab = lax.axis_index("slab")
    pencil = lax.axis_index("pencil")
    core, chip = pencil % CORES, pencil // CORES
    other = chip * CORES + 1 - core

    my_z, my_y = slab // 4, slab % 4

    slab_peers = [
        (slab // 4 + far_z) % 8 * 4 + (slab + far_y) % 4
        for far_z in (4, 3, 5, 2, 6, 1, 7, 0)
        for far_y in (2, 1, 3, 0)
        if far_z or far_y
    ]

    chunks = ROWS // CHUNK
    loads = []
    for c, (start, stop) in enumerate(LOADS):
        rows = pl.ds(start, stop - start)
        loads.append(
            [
                pltpu.make_async_copy(pre_hbm.at[rows], pre.at[rows], load_sem.at[0, c]),
                pltpu.make_async_copy(cot_hbm.at[rows], cot.at[rows], load_sem.at[1, c]),
                pltpu.make_async_copy(act_hbm.at[rows], act.at[rows], load_sem.at[2, c]),
            ]
        )
    kind = jnp.where(slab < 16, 0, jnp.where(pencil == 0, 2, 1))
    sources = (
        (xf_hbm, xf), (yf_hbm.at[pencil], yf), (zf_hbm.at[kind], zf), (zi_hbm.at[kind], zi), (tw_hbm, tw), (eo_hbm, eo), (ei_hbm, ei), (es_hbm, es),
        (yi_hbm.at[pencil], yi), (ye_hbm.at[pencil], ye), (xi_hbm, xi),
        (local_hbm, local_ref),
    )
    fetch = [pltpu.make_async_copy(a, b, table_sem.at[n]) for n, (a, b) in enumerate(sources)]
    by_name = dict(zip(TABLE_NAMES + ("local",), fetch))
    loads[0][0].start()
    loads[0][1].start()
    by_name["xf"].start()
    for load in loads[1:]:
        load[0].start()
        load[1].start()
    by_name["yf"].start()
    for load in loads:
        load[2].start()
    for name in by_name:
        if name not in ("xf", "yf"):
            by_name[name].start()

    barrier = pltpu.get_barrier_semaphore()

    @pl.loop(1, PENCILS)
    def _(j):
        pl.semaphore_signal(
            barrier, inc=1, device_id={"pencil": (pencil + j) % PENCILS}, device_id_type=pl.DeviceIdType.MESH
        )

    @pl.loop(1, SLABS)
    def _(j):
        pl.semaphore_signal(barrier, inc=1, device_id={"slab": (slab + j) % SLABS}, device_id_type=pl.DeviceIdType.MESH)

    def send_weights():
        @pl.loop(1, PENCILS)
        def _(j):
            d = (pencil + j) % PENCILS
            to_pencil(weight_hbm.at[pl.ds(2 * d, 2)], weights.at[pl.ds(4 * pencil, 2)], wsend, wrecv, d).start()

            @pl.when(d != 0)
            def _():
                to_pencil(
                    weight_hbm.at[pl.ds(31 - 2 * d, 2)], weights.at[pl.ds(4 * pencil + 2, 2)], wsend, wrecv, d
                ).start()

            @pl.when(d == 0)
            def _():
                to_pencil(weight_hbm.at[31], weights.at[4 * pencil + 2], wsend, wrecv, d).start()
                to_pencil(weight_hbm.at[16], weights.at[4 * pencil + 3], wsend, wrecv, d).start()

        for q in range(4):
            pltpu.make_async_copy(weight_hbm.at[y_index(pencil, q)], weights.at[4 * pencil + q], own_sem.at[q]).start()

    def gradient_values(step):
        for r in range(PAIR):
            y = step * PAIR + r
            for part in range(4):
                rows = pl.ds(part * (LANES // 4), LANES // 4)
                g = cot[y, rows].astype(F32) * gelu_slope(pre[y, rows].astype(F32))
                high, low = split(g)
                g_high[y, rows] = high
                g_low[y, rows] = low

    def store_modes(t, step, modes):
        for r in range(PAIR):
            place = (step * PAIR + r) * XROWS
            place = place if isinstance(place, int) else pl.multiple_of(place, 8)
            field_x[t, pl.ds(place, XROWS), :] = modes[:, r * LANES : (r + 1) * LANES]

    def gradient_modes(step):
        rows = pl.ds(step * PAIR, PAIR)
        both = product_t(xf[...], g_high[rows].reshape(PAIR * LANES, GRID))
        more = product_t(xf[:XPAD], g_low[rows].reshape(PAIR * LANES, GRID))
        store_modes(0, step, both[:XROWS] + both[XPAD : XPAD + XROWS] + more[:XROWS])

    for c, (start, stop) in enumerate(LOADS):
        loads[c][0].wait()
        loads[c][1].wait()
        if c == 0:
            by_name["xf"].wait()
            gradient_values(0)

        for step in range(max(start // PAIR, 1), stop // PAIR):
            gradient_modes(step - 1)
            gradient_values(step)
        if c == 2:
            pl.semaphore_wait(barrier, PENCILS - 1 + SLABS - 1)
            send_weights()

    gradient_modes(ROWS // PAIR - 1)

    def send_rows(t):
        out1[t, 0, BLOCK - 1] = jnp.zeros((8, LANES), F32)
        out1[t, 1, EDGE:BLOCK] = jnp.zeros((BLOCK - EDGE, 8, LANES), F32)
        for half, ks in enumerate((range(FIRST), range(FIRST, HALF))):
            for first in range(ks.start, ks.stop, 2):
                group = range(first, min(first + 2, ks.stop))
                columns = []
                for k in group:
                    real = field_x[t, pl.ds(k, ROWS, stride=XROWS), :]
                    imag = field_x[t, pl.ds(HALF + k, ROWS, stride=XROWS), :]
                    columns.append(jnp.concatenate([real, imag], axis=0))
                both = product(yf[...], stacked(jnp.concatenate(columns, axis=1)))
                for k in group:
                    modes = both[:, (k - first) * LANES : (k - first + 1) * LANES]
                    for d in range(PENCILS):
                        x = d // CORES
                        place = x * FIRST + k if k < FIRST else CHIPS * FIRST + x * REST + k - FIRST
                        out1[t, d % CORES, place] = modes[8 * d : 8 * d + 8]
                    out1[t, 0, EDGE + k // 4, 2 * (k % 4) : 2 * (k % 4) + 2] = modes[64:66]
            pair_copy(t, half).start()

    def pair_copy(t, half):
        tiles = pl.ds(0, CHIPS * FIRST) if half == 0 else pl.ds(CHIPS * FIRST, BLOCK - CHIPS * FIRST)
        return to_pencil(
            out1.at[t, 1 - core, tiles], pair_in.at[t, tiles], psend.at[t], precv.at[t, half], other
        )

    halves = (first_tiles, rest_tiles)
    spans = (pl.ds(0, FIRST), pl.ds(FIRST, REST))

    def x_copy(t, half, to, source):
        return to_pencil(
            sum1.at[t, halves[half](to)], in1.at[t, source, spans[half]], send1.at[t, half], recv1.at[t, source, half],
            to * CORES + core,
        )

    def send_sums(t):
        for half in range(2):
            pair_copy(t, half).wait_recv()
            for j in (2, 1, 3, 0):
                x = (chip + j) % CHIPS
                tiles = halves[half](x)
                sum1[t, tiles] = out1[t, core, tiles] + pair_in[t, tiles]
                if j:
                    x_copy(t, half, x, chip).start()
        sum1[t, EDGE:BLOCK] = out1[t, core, EDGE:BLOCK] + pair_in[t, EDGE:BLOCK]

        @pl.when((core == 0) & (chip != 0))
        def _():
            to_pencil(
                sum1.at[t, pl.ds(EDGE, BLOCK - EDGE)], edge_in.at[t, chip], esend.at[t], erecv.at[t, chip], 0
            ).start()

    by_name["yf"].wait()
    send_rows(0)
    send_sums(0)

    for c, (start, stop) in enumerate(LOADS):
        loads[c][2].wait()

        @pl.loop(start // PAIR, stop // PAIR, unroll=True)
        def _(step):
            both = product_t(xf[...], act[pl.ds(step * PAIR, PAIR)].reshape(PAIR * LANES, GRID))
            store_modes(1, step, both[:XROWS] + both[XPAD : XPAD + XROWS])

    send_rows(1)
    lane = lax.broadcasted_iota(jnp.int32, (LANES, LANES), 1) // CHAN
    row = lax.broadcasted_iota(jnp.int32, (LANES, LANES), 0) // CHAN

    def send_tiles(t):
        for half, ks in enumerate((range(FIRST), range(FIRST, HALF))):
            total = sum1[t, halves[half](chip)]
            for j in range(1, CHIPS):
                x = (chip + j) % CHIPS
                x_copy(t, half, x, x).wait_recv()
                total = total + in1[t, x, spans[half]]
            for k in ks:
                if k < 16:
                    out2[t, k] = total[k - ks.start]
                if k > 0:
                    out2[t, MODES - k] = total[k - ks.start]

        @pl.when(pencil == 0)
        def _():
            edge = sum1[t, EDGE:BLOCK]
            for x in range(1, CHIPS):
                to_pencil(
                    sum1.at[t, pl.ds(EDGE, BLOCK - EDGE)], edge_in.at[t, x], esend.at[t], erecv.at[t, x], 0
                ).wait_recv()
                edge = edge + edge_in[t, x]
            for k in range(1, HALF):
                r = 2 * (k % 4)
                out2[t, MODES - k, 3:4] = edge[k // 4, r : r + 1]
                out2[t, MODES - k, 7:8] = edge[k // 4, r + 1 : r + 2]

        for d in slab_peers:
            to_slab(out2.at[t, d], in2.at[t, slab], send2.at[t], recv2.at[t], d).start()

        in2[t, slab] = out2[t, slab]

    send_sums(1)
    send_tiles(0)

    sums_acc[...] = jnp.zeros_like(sums_acc)

    @pl.loop(0, ROWS, step=4, unroll=True)
    def _(first):
        left, right = [], []
        for r in range(4):
            left.append(jnp.concatenate([g_high[first + r], g_low[first + r]], axis=0))
            right.append(act[first + r])
        sums_acc[...] += product_t(jnp.concatenate(left, axis=1), jnp.concatenate(right, axis=1))

    full = jnp.where(lane == row, sums_acc[:LANES] + sums_acc[LANES:], 0.0)
    full = jnp.sum(full.reshape(PLANES, CHAN, LANES), axis=0)
    for shift in (CHAN, 2 * CHAN, 4 * CHAN):
        full = full + pltpu.roll(full, shift, 1)
    o_row = lax.broadcasted_iota(jnp.int32, (CHAN, LANES), 0) % 8
    o_lane = lax.broadcasted_iota(jnp.int32, (CHAN, LANES), 1) // CHAN
    full = jnp.where(o_row == o_lane, full, 0.0).reshape(2, 8, LANES)
    full = jnp.sum(full, axis=1, keepdims=True)
    place = lax.broadcasted_iota(jnp.int32, (8, LANES), 0)
    sums_mine[...] = jnp.where(place == 0, full[0], jnp.where(place == 1, full[1], 0.0))

    @pl.loop(1, PENCILS)
    def _(j):
        d = (pencil + j) % PENCILS
        to_pencil(sums_mine, sums_a.at[pencil], asend, arecv.at[pencil], d).start()

    for name in TABLE_NAMES[2:]:
        by_name[name].wait()

    mode_tiles = (MODE_ROWS // 8, 8, LANES)
    place = lax.broadcasted_iota(jnp.int32, mode_tiles, 1)
    first_part = place % 2 == 0
    first_half = place % 4 < 2

    def z_product(table, value):
        high, low = split(value)
        both = product(table[0], jnp.concatenate([high, low], axis=1))
        return both[:, :LANES] + both[:, LANES:] + product(table[1], high)

    def modes_of(t, expand):
        most = pl.ds(0, SLABS - 1)
        to_slab(out2.at[t, most], in2.at[t, most], send2.at[t], recv2.at[t], slab).wait_recv()
        found = z_product(zf, in2[t].reshape(256, LANES)).reshape(mode_tiles)
        found = found * tw[0] + parts_swapped(found) * tw[1]
        high, low = split(found.reshape(MODE_ROWS, LANES))
        wide = product(jnp.concatenate([high, low], axis=1), expand)
        return jnp.where(first_half, wide[:, :LANES].reshape(mode_tiles), wide[:, LANES:].reshape(mode_tiles))

    def both_parts(tile):
        swapped = parts_swapped(tile)
        return jnp.where(first_part, tile, swapped), jnp.where(first_part, swapped, tile)

    to_pencil(
        weight_hbm.at[pl.ds(0, 28)], weights.at[pl.ds(0, 28)], wsend, wrecv, pencil
    ).wait_recv()
    for q in range(4):
        pltpu.make_async_copy(weight_hbm.at[y_index(pencil, q)], weights.at[4 * pencil + q], own_sem.at[q]).wait()
    weight_parts[0], weight_parts[1] = both_parts(weights[...].reshape(mode_tiles))

    send_tiles(1)

    lower = modes_of(0, eo[...])
    swapped = parts_swapped(lower)
    turned = jnp.where(first_part, swapped, -swapped)
    low_modes[0] = lower
    low_modes[1] = turned
    high, low = split((weight_parts[0] * lower + weight_parts[1] * turned).reshape(MODE_ROWS, LANES))
    back = product(jnp.concatenate([high, low], axis=1), es[...]).reshape(mode_tiles)
    back = back * tw[0] - parts_swapped(back) * tw[1]
    out3[...] = z_product(zi, back.reshape(MODE_ROWS, LANES)).reshape(SLABS, 8, LANES)

    for d in slab_peers:
        to_slab(out3.at[d], in3.at[slab], send3, recv3, d).start()

    in3[slab] = out3[slab]

    upper = modes_of(1, ei[...])
    real, imag = both_parts(upper)
    grads[...] = (low_modes[0] * real + low_modes[1] * imag).reshape(MODES, 16, LANES)

    @pl.loop(1, PENCILS)
    def _(j):
        d = (pencil + j) % PENCILS
        to_pencil(grads.at[pl.ds(4 * d, 2)], grad_hbm.at[pl.ds(2 * pencil, 2)], gsend, grecv, d).start()

        @pl.when(pencil != 0)
        def _():
            to_pencil(
                grads.at[pl.ds(4 * d + 2, 2)], grad_hbm.at[pl.ds(31 - 2 * pencil, 2)], gsend, grecv, d
            ).start()

        @pl.when(pencil == 0)
        def _():
            to_pencil(grads.at[4 * d + 2], grad_hbm.at[31], gsend, grecv, d).start()
            to_pencil(grads.at[4 * d + 3], grad_hbm.at[16], gsend, grecv, d).start()

    for q in range(4):
        pltpu.make_async_copy(grads.at[4 * pencil + q], grad_hbm.at[y_index(pencil, q)], own_sem.at[4 + q]).start()

    sums_a[pencil] = sums_mine[...]
    for j in range(1, PENCILS):
        d = (pencil + j) % PENCILS
        to_pencil(sums_mine, sums_a.at[d], asend, arecv.at[d], d).wait_recv()
    total = jnp.zeros((8, LANES), F32)
    for d in range(PENCILS):
        total = total + sums_a[d]
    sums_y[my_y] = total
    for j in range(1, 4):
        to_slab(sums_y.at[my_y], sums_y.at[my_y], ysend, yrecv, my_z * 4 + (my_y + j) % 4).start()

    def back_copy(half, p, to, sem):
        return to_pencil(out4.at[spans[half]], in4.at[p, spans[half]], sem, recv4.at[p, half], to)

    to_slab(out3.at[pl.ds(0, SLABS - 1)], in3.at[pl.ds(0, SLABS - 1)], send3, recv3, slab).wait_recv()
    for half, ks in enumerate((range(FIRST), range(FIRST, HALF))):
        for k in ks:
            out4[k] = in3[k] + in3[MODES - k] if 0 < k < 16 else in3[k]

        @pl.when(pencil == 0)
        def _():
            for k in ks:
                for part in range(2):
                    r = 3 + 4 * part
                    if k > 0:
                        edge4[2 * k + part : 2 * k + part + 1] = in3[MODES - k, r : r + 1]
                        out4[k, r : r + 1] = in3[k, r : r + 1] if k < 16 else jnp.zeros((1, LANES), F32)

        for j in (2, 1, 3):
            x = (chip + j) % CHIPS
            back_copy(half, pencil, x * CORES + core, send4.at[half]).start()
        back_copy(half, pencil, other, send4.at[2]).start()

    @pl.when(pencil == 0)
    def _():
        edge4[0:2] = jnp.zeros((2, LANES), F32)
        edge4[34:40] = jnp.zeros((6, LANES), F32)

        @pl.loop(1, PENCILS)
        def _(d):
            to_pencil(edge4, edge4, xsend, xrecv, d).start()

    in4[pencil] = out4[...]

    pick = jnp.where(
        lax.broadcasted_iota(jnp.int32, (LANES, CHAN), 0) % CHAN == lax.broadcasted_iota(jnp.int32, (LANES, CHAN), 1),
        1.0,
        0.0,
    )
    by_name["local"].wait()
    mixed = exact_product(pick, local_ref[...], ((1,), (1,)))
    mixed = exact_product(mixed, pick, ((1,), (1,)))
    mix_high, mix_low = split(jnp.where(lane == row, mixed, 0.0))
    mix_rows = jnp.concatenate([mix_high, mix_high], axis=1)
    mix_more = jnp.concatenate([mix_low, jnp.zeros_like(mix_low)], axis=1)
    mix[...] = jnp.concatenate([mix_rows, mix_more], axis=0)

    @pl.loop(0, ROWS, unroll=4)
    def _(y):
        both = product(mix[...], jnp.concatenate([g_high[y], g_low[y]], axis=0))
        local_part[y] = both[:LANES] + both[LANES:]

    to_slab(sums_y.at[pl.ds(0, 3)], sums_y.at[pl.ds(0, 3)], ysend, yrecv, slab).wait_recv()
    total = sums_y[0]
    for j in range(1, 4):
        total = total + sums_y[j]
    sums_z[my_z] = total
    for j in range(1, 8):
        to_slab(sums_z.at[my_z], sums_z.at[my_z], zsend, zrecv, (my_z + j) % 8 * 4 + my_y).start()

    for half in range(2):
        for j in (1, 3, 2):
            d = (chip + j) % CHIPS * CORES + core
            back_copy(half, d, d, send4.at[half]).wait_recv()
            to_pencil(
                in4.at[d, spans[half]], in4.at[d, spans[half]], fsend.at[half], recv4.at[d, half], other
            ).start()

    @pl.when(pencil != 0)
    def _():
        to_pencil(edge4, edge4, xsend, xrecv, 0).wait_recv()

    spread_y[pl.ds(2 * HALF * ROWS, (XROWS - 2 * HALF) * ROWS), :] = jnp.zeros(((XROWS - 2 * HALF) * ROWS, LANES), F32)
    for half, ks in enumerate((range(FIRST), range(FIRST, HALF))):
        for x in range(CHIPS):
            back_copy(half, x * CORES + 1 - core, other, send4.at[2]).wait_recv()
        for first in range(ks.start, ks.stop, 2):
            group = range(first, min(first + 2, ks.stop))
            columns = [jnp.concatenate([in4[p, k] for p in range(PENCILS)], axis=0) for k in group]
            both = product(yi[...], stacked(jnp.concatenate(columns, axis=1)))
            for k in group:
                field = both[:, (k - first) * LANES : (k - first + 1) * LANES]
                edge_real, edge_imag = edge4[2 * k : 2 * k + 1], edge4[2 * k + 1 : 2 * k + 2]
                spread_y[k * ROWS : (k + 1) * ROWS] = field[:ROWS] + ye[0] * edge_real - ye[1] * edge_imag
                spread_y[(HALF + k) * ROWS : (HALF + k + 1) * ROWS] = (
                    field[ROWS:] + ye[0] * edge_imag + ye[1] * edge_real
                )

    to_slab(sums_z.at[pl.ds(0, 7)], sums_z.at[pl.ds(0, 7)], zsend, zrecv, slab).wait_recv()
    total = sums_z[0]
    for j in range(1, 8):
        total = total + sums_z[j]
    sums_all[...] = total * float(GRID) ** -1.5
    stores = [pltpu.make_async_copy(sums_all, sum_hbm, store_sem.at[chunks])]
    stores[0].start()

    for c in range(chunks):

        columns = []
        for r in range(CHUNK):
            value = spread_y[pl.ds(c * CHUNK + r, XROWS, stride=ROWS), :]
            high = value.astype(BF16).astype(F32)
            column = jnp.concatenate([high, value - high, high, jnp.zeros((8, LANES), F32)], axis=0)
            columns.append(column.T.astype(BF16))
        fields = product(jnp.concatenate(columns, axis=0), xi[...])
        for r in range(CHUNK):
            y = c * CHUNK + r
            result[y] = (local_part[y] + fields[r * LANES : (r + 1) * LANES]).astype(BF16)

        rows = pl.ds(c * CHUNK, CHUNK)
        stores.append(pltpu.make_async_copy(result.at[rows], result_hbm.at[rows], store_sem.at[c]))
        stores[-1].start()

    to_pencil(weights.at[pl.ds(0, 28)], weights.at[pl.ds(0, 28)], wsend, wrecv, pencil).wait_send()
    for t in range(2):
        to_pencil(out1.at[t, 1 - core], pair_in.at[t], psend.at[t], precv.at[t, 0], other).wait_send()
        for half in range(2):
            some = in1.at[t, pl.ds(0, 3), spans[half]]
            to_pencil(some, some, send1.at[t, half], recv1.at[t, 0, half], other).wait_send()
        most = pl.ds(0, SLABS - 1)
        to_slab(out2.at[t, most], in2.at[t, most], send2.at[t], recv2.at[t], slab).wait_send()

        @pl.when((core == 0) & (chip != 0))
        def _():
            to_pencil(
                sum1.at[t, pl.ds(EDGE, BLOCK - EDGE)], edge_in.at[t, chip], esend.at[t], erecv.at[t, chip], 0
            ).wait_send()

    to_pencil(sums_a.at[pl.ds(0, 7)], sums_a.at[pl.ds(0, 7)], asend, arecv.at[0], pencil).wait_send()
    to_slab(sums_y.at[pl.ds(0, 3)], sums_y.at[pl.ds(0, 3)], ysend, yrecv, slab).wait_send()
    to_slab(sums_z.at[pl.ds(0, 7)], sums_z.at[pl.ds(0, 7)], zsend, zrecv, slab).wait_send()
    to_slab(out3.at[pl.ds(0, 31)], in3.at[pl.ds(0, 31)], send3, recv3, slab).wait_send()
    for half in range(2):
        some = in4.at[pl.ds(0, 3), spans[half]]
        to_pencil(some, some, send4.at[half], recv4.at[0, half], other).wait_send()
        to_pencil(some, some, fsend.at[half], recv4.at[0, half], other).wait_send()
    to_pencil(out4, in4.at[pencil], send4.at[2], recv4.at[pencil, 0], other).wait_send()

    @pl.when(pencil == 0)
    def _():
        for d in range(1, PENCILS):
            to_pencil(edge4, edge4, xsend, xrecv, d).wait_send()

    to_pencil(grads.at[pl.ds(0, 28)], grad_hbm.at[pl.ds(0, 28)], gsend, grecv, pencil).wait()
    for q in range(4):
        pltpu.make_async_copy(grads.at[4 * pencil + q], grad_hbm.at[y_index(pencil, q)], own_sem.at[4 + q]).wait()
    for store in stores:
        store.wait()


def last_kernel(
    result_hbm, grad_in, sum_hbm,
    out_hbm, local_hbm, grad_out,
    result, grad, sum_ref, local_ref, load_sem, store_sem,
):
    rows = [pl.ds(c * (ROWS // PARTS), ROWS // PARTS) for c in range(PARTS)]
    loads = [pltpu.make_async_copy(result_hbm.at[r], result.at[r], load_sem.at[c]) for c, r in enumerate(rows)]
    stores = [pltpu.make_async_copy(result.at[r], out_hbm.at[r], store_sem.at[c]) for c, r in enumerate(rows)]
    loads.append(pltpu.make_async_copy(grad_in, grad, load_sem.at[PARTS]))
    stores.append(pltpu.make_async_copy(grad, grad_out, store_sem.at[PARTS]))
    load_sum = pltpu.make_async_copy(sum_hbm, sum_ref, load_sem.at[PARTS + 1])
    load_sum.start()
    for load in loads:
        load.start()

    o_row = lax.broadcasted_iota(jnp.int32, (CHAN, LANES), 0)
    o_lane = lax.broadcasted_iota(jnp.int32, (CHAN, LANES), 1)
    load_sum.wait()
    total = jnp.where(o_row < 8, sum_ref[0:1], sum_ref[1:2])
    total = jnp.where(o_row % 8 == o_lane // CHAN, total, 0.0)
    pick = jnp.where(
        lax.broadcasted_iota(jnp.int32, (LANES, CHAN), 0) % CHAN == lax.broadcasted_iota(jnp.int32, (LANES, CHAN), 1),
        1.0,
        0.0,
    )
    local_ref[...] = exact_product(total, pick, ((1,), (0,)))
    store_local = pltpu.make_async_copy(local_ref, local_hbm, store_sem.at[PARTS + 1])
    store_local.start()
    for load, store in zip(loads, stores):
        load.wait()
        store.start()
    for store in stores:
        store.wait()
    store_local.wait()


def on_device(activation, preact, cotangent, local_weight, spectral_weight):
    made = tables()
    fields = [a.reshape(ROWS, LANES, GRID) for a in (activation, preact, cotangent)]
    weight = spectral_weight[0].reshape(MODES, 4, 2, 2, LANES).transpose(0, 1, 3, 2, 4).reshape(MODES, 16, LANES)
    any_space = pl.BlockSpec(memory_space=pl.ANY)
    dma = pltpu.SemaphoreType.DMA
    field = pltpu.VMEM((ROWS, LANES, GRID), BF16)
    wide_field = pltpu.VMEM((ROWS, LANES, GRID), F32)
    tile = (8, LANES)
    result, grad, total = pl.pallas_call(
        modes_kernel,
        out_shape=(
            jax.ShapeDtypeStruct((ROWS, LANES, GRID), BF16),
            jax.ShapeDtypeStruct((MODES, 16, LANES), F32),
            jax.ShapeDtypeStruct(tile, F32),
        ),
        in_specs=[any_space] * (5 + len(TABLE_NAMES)),
        out_specs=(any_space, any_space, any_space),
        scratch_shapes=[
            field, field, field, field, field, wide_field, field,
            pltpu.VMEM((2 * XPAD, GRID), BF16),
            pltpu.VMEM((80, 192), BF16),
            pltpu.VMEM((2, MODE_ROWS, 256), BF16),
            pltpu.VMEM((2, 256, MODE_ROWS), BF16),
            pltpu.VMEM((2, MODE_ROWS // 8, 8, LANES), F32),
            pltpu.VMEM((256, 256), BF16),
            pltpu.VMEM((256, 256), BF16),
            pltpu.VMEM((256, LANES), BF16),
            pltpu.VMEM((64, 192), BF16),
            pltpu.VMEM((2, ROWS, LANES), F32),
            pltpu.VMEM((128, GRID), BF16),
            pltpu.VMEM((2, ROWS * XROWS, LANES), F32),
            pltpu.VMEM((ROWS * XROWS, LANES), F32),
            pltpu.VMEM((2, CORES, BLOCK) + tile, F32),
            pltpu.VMEM((2, BLOCK) + tile, F32),
            pltpu.VMEM((2, BLOCK) + tile, F32),
            pltpu.VMEM((2, CHIPS, HALF) + tile, F32),
            pltpu.VMEM((2, CHIPS, BLOCK - EDGE) + tile, F32),
            pltpu.VMEM((2, SLABS) + tile, F32),
            pltpu.VMEM((2, SLABS) + tile, F32),
            pltpu.VMEM((MODES, 16, LANES), F32),
            pltpu.VMEM((2, MODE_ROWS // 8, 8, LANES), F32),
            pltpu.VMEM((2, MODE_ROWS // 8, 8, LANES), F32),
            pltpu.VMEM((SLABS,) + tile, F32),
            pltpu.VMEM((SLABS,) + tile, F32),
            pltpu.VMEM((HALF,) + tile, F32),
            pltpu.VMEM((PENCILS, HALF) + tile, F32),
            pltpu.VMEM((XROWS, LANES), F32),
            pltpu.VMEM((MODES, 16, LANES), F32),
            pltpu.VMEM((2 * LANES, LANES), F32),
            pltpu.VMEM((PENCILS,) + tile, F32),
            pltpu.VMEM((4,) + tile, F32),
            pltpu.VMEM((8,) + tile, F32),
            pltpu.VMEM(tile, F32),
            pltpu.VMEM(tile, F32),
            pltpu.VMEM((CHAN, CHAN), F32),
            pltpu.VMEM((2 * LANES, 2 * LANES), BF16),
            dma((len(TABLE_NAMES) + 1,)), dma((3, len(LOADS))), dma((ROWS // CHUNK + 1,)), dma((8,)),
            dma((2,)), dma((2, 2)), dma((2, 2)), dma((2, CHIPS, 2)), dma((2,)), dma((2, CHIPS)),
            dma((2,)), dma((2,)), dma, dma,
            dma, dma, dma((3,)), dma((PENCILS, 2)), dma((2,)), dma, dma, dma, dma,
            dma, dma((PENCILS,)), dma, dma, dma, dma,
        ],
        compiler_params=pltpu.CompilerParams(
            collective_id=0, has_side_effects=True, vmem_limit_bytes=62 * 1024 * 1024
        ),
        cost_estimate=pl.CostEstimate(flops=3_000_000_000, bytes_accessed=11_000_000, transcendentals=2_000_000),
        name="modes",
    )(*fields, weight, local_weight, *(jnp.asarray(made[name]) for name in TABLE_NAMES))
    out, grad_local, grad_spectral = pl.pallas_call(
        last_kernel,
        out_shape=(
            jax.ShapeDtypeStruct((ROWS, LANES, GRID), BF16),
            jax.ShapeDtypeStruct((CHAN, CHAN), F32),
            jax.ShapeDtypeStruct((MODES, 16, LANES), F32),
        ),
        in_specs=[any_space, any_space, any_space],
        out_specs=(any_space, any_space, any_space),
        scratch_shapes=[
            field,
            pltpu.VMEM((MODES, 16, LANES), F32),
            pltpu.VMEM(tile, F32),
            pltpu.VMEM((CHAN, CHAN), F32),
            dma((PARTS + 2,)), dma((PARTS + 2,)),
        ],
        compiler_params=pltpu.CompilerParams(vmem_limit_bytes=62 * 1024 * 1024),
        cost_estimate=pl.CostEstimate(flops=100_000, bytes_accessed=5_000_000, transcendentals=0),
        name="last",
    )(result, grad, total)
    grad_spectral = grad_spectral.reshape(MODES, 4, 2, 2, LANES).transpose(0, 1, 3, 2, 4).reshape(spectral_weight.shape)
    return out.reshape(activation.shape), grad_local, grad_spectral


def solution(mesh):
    field = P("pencil", "slab", None, None)
    modes = P("slab", None, "pencil", None, None)
    return jax.shard_map(
        on_device,
        mesh=mesh,
        in_specs=(field, field, field, P(), modes),
        out_specs=(field, P(), modes),
        check_vma=False,
    )
```

```python
import functools

import jax
import jax.numpy as jnp
import ml_dtypes
import numpy as np
from jax import lax
from jax.experimental import pallas as pl
from jax.experimental.pallas import tpu as pltpu
from jax.sharding import PartitionSpec as P

GRID = 256
CHAN = 16
MODES = 32
SLABS = 32
PENCILS = 8
ROWS = GRID // PENCILS
PLANES = GRID // SLABS
LANES = PLANES * CHAN
HALF = MODES // 2 + 1
XROWS = 40
XPAD = 48
CORES = 2
CHIPS = PENCILS // CORES
FIRST = 9
REST = HALF - FIRST
EDGE = CHIPS * HALF
BLOCK = EDGE + XROWS // 8
PARTS = 8
MODE_ROWS = 512
CHUNK = 8
LOADS = ((0, 4), (4, 8), (8, 16), (16, 24), (24, 32))
PAIR = 2
F32 = jnp.float32
BF16 = jnp.bfloat16


def kept(j):
    return np.where(j < MODES // 2, j, j - MODES)


def y_set(p):
    if p == 0:
        return np.array([0, 1, -1, -16])
    return np.array([2 * p, 2 * p + 1, -2 * p - 1, -2 * p])


def pieces(table):
    high = table.astype(np.float32).astype(ml_dtypes.bfloat16)
    low = (table - high.astype(np.float64)).astype(np.float32).astype(ml_dtypes.bfloat16)
    return high, low


def turn(freq, position):
    angle = 2.0 * np.pi * ((freq * position) % GRID) / GRID
    return np.cos(angle), np.sin(angle)


@functools.cache
def tables():
    made = {}
    cells = np.arange(GRID)

    cosine, sine = turn(np.arange(HALF)[:, None], cells[None, :])
    forward_x = np.zeros((XPAD, GRID))
    forward_x[:HALF], forward_x[HALF : 2 * HALF] = cosine, -sine
    made["xf"] = np.concatenate(pieces(forward_x), axis=0)
    high, low = pieces(forward_x[:XROWS])
    made["xi"] = np.concatenate([high, high, low, np.zeros((8, GRID), high.dtype)], axis=0)

    forward_y = np.zeros((PENCILS, 80, 2, ROWS))
    inverse_y = np.zeros((PENCILS, 2, ROWS, PENCILS, 2, 4))
    extra_y = np.zeros((PENCILS, 2, ROWS, LANES))
    for p in range(PENCILS):
        rows = p * ROWS + np.arange(ROWS)
        for d in range(PENCILS):
            cosine, sine = turn(y_set(d)[:, None], rows[None, :])
            forward_y[p, 8 * d : 8 * d + 4, 0], forward_y[p, 8 * d : 8 * d + 4, 1] = cosine, sine
            forward_y[p, 8 * d + 4 : 8 * d + 8, 0], forward_y[p, 8 * d + 4 : 8 * d + 8, 1] = -sine, cosine
            inverse_y[p, 0, :, d, 0], inverse_y[p, 0, :, d, 1] = cosine.T, -sine.T
            inverse_y[p, 1, :, d, 0], inverse_y[p, 1, :, d, 1] = sine.T, cosine.T
        cosine, sine = turn(16, rows)
        forward_y[p, 64, 0], forward_y[p, 64, 1] = cosine, sine
        forward_y[p, 65, 0], forward_y[p, 65, 1] = -sine, cosine
        extra_y[p, 0], extra_y[p, 1] = cosine[:, None], sine[:, None]
    high, low = pieces(forward_y.reshape(PENCILS, 80, 2 * ROWS))
    made["yf"] = np.concatenate([high, high, low], axis=2)
    high, low = pieces(inverse_y.reshape(PENCILS, 2 * ROWS, 64))
    made["yi"] = np.concatenate([high, high, low], axis=2)
    made["ye"] = extra_y.astype(np.float32)

    z_freq = kept(np.arange(MODES)).reshape(8, 4)
    slab = np.arange(SLABS)
    cosine, sine = turn(z_freq[:, :, None], 8 * slab[None, None, :])
    cosine, sine = cosine[:, :, None, :], sine[:, :, None, :]
    forward_z = np.zeros((8, 4, 4, 2, 2, SLABS, 2, 4))
    for q in range(4):
        forward_z[:, q, :, :, 0, :, 0, q], forward_z[:, q, :, :, 0, :, 1, q] = cosine, sine
        forward_z[:, q, :, :, 1, :, 0, q], forward_z[:, q, :, :, 1, :, 1, q] = -sine, cosine
    forward_z = forward_z.reshape(MODE_ROWS, SLABS, 8)
    kinds = [forward_z]
    for order in ([3, 2, 1, 0], [0, 2, 1, 3]):
        mirrored = np.zeros_like(forward_z)
        for q in range(4):
            mirrored[:, :, order[q]] = forward_z[:, :, q]
            mirrored[:, :, 4 + order[q]] = -forward_z[:, :, 4 + q]
        kinds.append(mirrored)
    kinds = np.stack(kinds).reshape(3, MODE_ROWS, 256)
    made["zf"] = np.stack(pieces(kinds), axis=1)
    made["zi"] = np.stack(pieces(kinds.transpose(0, 2, 1)), axis=1)
    cosine, sine = turn(z_freq[:, :, None], np.arange(PLANES)[None, None, :])
    spread = np.zeros((2, 8, 4, 4, 2, 2, PLANES, CHAN))
    spread[0] = cosine[:, None, :, None, None, :, None]
    spread[1, :, :, :, :, 0] = sine[:, None, :, None, :, None]
    spread[1, :, :, :, :, 1] = -sine[:, None, :, None, :, None]
    made["tw"] = spread.reshape(2, MODE_ROWS // 8, 8, LANES).astype(np.float32)

    same = np.eye(CHAN)
    of_output = np.broadcast_to(same[None, :, :, None], (PLANES, CHAN, CHAN, CHAN)).reshape(LANES, 256)
    of_input = np.broadcast_to(same[None, :, None, :], (PLANES, CHAN, CHAN, CHAN)).reshape(LANES, 256)
    made["eo"] = (np.concatenate([of_output, of_output]) * float(GRID) ** -3).astype(ml_dtypes.bfloat16)
    made["ei"] = np.concatenate([of_input, of_input]).astype(ml_dtypes.bfloat16)
    made["es"] = np.concatenate([of_input.T[:LANES]] * 2).astype(ml_dtypes.bfloat16)
    return made


TABLE_NAMES = ("xf", "yf", "zf", "zi", "tw", "eo", "ei", "es", "yi", "ye", "xi")


def product(a, b):
    return lax.dot_general(a, b, (((1,), (0,)), ((), ())), preferred_element_type=F32)


def product_t(a, b):
    return lax.dot_general(a, b, (((1,), (1,)), ((), ())), preferred_element_type=F32)


def exact_product(a, b, dims):
    return lax.dot_general(a, b, (dims, ((), ())), precision=lax.Precision.HIGHEST, preferred_element_type=F32)


def split(value):
    high = value.astype(BF16)
    return high, (value - high.astype(F32)).astype(BF16)


def stacked(value):
    high, low = split(value)
    return jnp.concatenate([high, low, high], axis=0)


def gelu_slope(value):
    normal_cdf = 0.5 * (1.0 + lax.erf(value * 0.7071067811865476))
    density = jnp.exp(-0.5 * value * value) * 0.3989422804014327
    return normal_cdf + value * density


def parts_swapped(tile):
    even = lax.broadcasted_iota(jnp.int32, tile.shape, 1) % 2 == 0
    return jnp.where(even, pltpu.roll(tile, 7, 1), pltpu.roll(tile, 1, 1))


def to_pencil(src, dst, send, recv, d):
    return pltpu.make_async_remote_copy(
        src_ref=src,
        dst_ref=dst,
        send_sem=send,
        recv_sem=recv,
        device_id={"pencil": d},
        device_id_type=pl.DeviceIdType.MESH,
    )


def to_slab(src, dst, send, recv, d):
    return pltpu.make_async_remote_copy(
        src_ref=src,
        dst_ref=dst,
        send_sem=send,
        recv_sem=recv,
        device_id={"slab": d},
        device_id_type=pl.DeviceIdType.MESH,
    )


def first_tiles(x):
    return pl.ds(x * FIRST, FIRST)


def rest_tiles(x):
    return pl.ds(CHIPS * FIRST + x * REST, REST)


def y_index(p, q):
    if q < 2:
        return 2 * p + q
    if q == 2:
        return 31 - 2 * p
    return jnp.where(p == 0, 16, 32 - 2 * p)


def modes_kernel(
    act_hbm, pre_hbm, cot_hbm, weight_hbm, local_hbm,
    xf_hbm, yf_hbm, zf_hbm, zi_hbm, tw_hbm, eo_hbm, ei_hbm, es_hbm, yi_hbm, ye_hbm, xi_hbm,
    result_hbm, grad_hbm, sum_hbm,
    act, pre, cot, g_high, g_low, local_part, result,
    xf, yf, zf, zi, tw, eo, ei, es, yi, ye, xi,
    field_x, spread_y,
    out1, pair_in, sum1, in1, edge_in, out2, in2,
    weights, weight_parts, low_modes, out3, in3, out4, in4, edge4, grads,
    sums_acc, sums_a, sums_y, sums_z, sums_mine, sums_all, local_ref, mix,
    table_sem, load_sem, store_sem, own_sem,
    psend, precv, send1, recv1, esend, erecv, send2, recv2, wsend, wrecv,
    send3, recv3, send4, recv4, fsend, xsend, xrecv, gsend, grecv,
    asend, arecv, ysend, yrecv, zsend, zrecv,
):
    slab = lax.axis_index("slab")
    pencil = lax.axis_index("pencil")
    core, chip = pencil % CORES, pencil // CORES
    other = chip * CORES + 1 - core

    my_z, my_y = slab // 4, slab % 4

    slab_peers = [
        (slab // 4 + far_z) % 8 * 4 + (slab + far_y) % 4
        for far_z in (4, 3, 5, 2, 6, 1, 7, 0)
        for far_y in (2, 1, 3, 0)
        if far_z or far_y
    ]

    chunks = ROWS // CHUNK
    loads = []
    for c, (start, stop) in enumerate(LOADS):
        rows = pl.ds(start, stop - start)
        loads.append(
            [
                pltpu.make_async_copy(pre_hbm.at[rows], pre.at[rows], load_sem.at[0, c]),
                pltpu.make_async_copy(cot_hbm.at[rows], cot.at[rows], load_sem.at[1, c]),
                pltpu.make_async_copy(act_hbm.at[rows], act.at[rows], load_sem.at[2, c]),
            ]
        )
    kind = jnp.where(slab < 16, 0, jnp.where(pencil == 0, 2, 1))
    sources = (
        (xf_hbm, xf), (yf_hbm.at[pencil], yf), (zf_hbm.at[kind], zf), (zi_hbm.at[kind], zi), (tw_hbm, tw), (eo_hbm, eo), (ei_hbm, ei), (es_hbm, es),
        (yi_hbm.at[pencil], yi), (ye_hbm.at[pencil], ye), (xi_hbm, xi),
        (local_hbm, local_ref),
    )
    fetch = [pltpu.make_async_copy(a, b, table_sem.at[n]) for n, (a, b) in enumerate(sources)]
    by_name = dict(zip(TABLE_NAMES + ("local",), fetch))
    loads[0][0].start()
    loads[0][1].start()
    by_name["xf"].start()
    for load in loads[1:]:
        load[0].start()
        load[1].start()
    by_name["yf"].start()
    for load in loads:
        load[2].start()
    for name in by_name:
        if name not in ("xf", "yf"):
            by_name[name].start()

    barrier = pltpu.get_barrier_semaphore()

    @pl.loop(1, PENCILS)
    def _(j):
        pl.semaphore_signal(
            barrier, inc=1, device_id={"pencil": (pencil + j) % PENCILS}, device_id_type=pl.DeviceIdType.MESH
        )

    @pl.loop(1, SLABS)
    def _(j):
        pl.semaphore_signal(barrier, inc=1, device_id={"slab": (slab + j) % SLABS}, device_id_type=pl.DeviceIdType.MESH)

    def gradient_values(step):
        for r in range(PAIR):
            y = step * PAIR + r
            for part in range(4):
                rows = pl.ds(part * (LANES // 4), LANES // 4)
                g = cot[y, rows].astype(F32) * gelu_slope(pre[y, rows].astype(F32))
                high, low = split(g)
                g_high[y, rows] = high
                g_low[y, rows] = low

    def store_modes(t, step, modes):
        for r in range(PAIR):
            place = (step * PAIR + r) * XROWS
            place = place if isinstance(place, int) else pl.multiple_of(place, 8)
            field_x[t, pl.ds(place, XROWS), :] = modes[:, r * LANES : (r + 1) * LANES]

    def gradient_modes(step):
        rows = pl.ds(step * PAIR, PAIR)
        both = product_t(xf[...], g_high[rows].reshape(PAIR * LANES, GRID))
        more = product_t(xf[:XPAD], g_low[rows].reshape(PAIR * LANES, GRID))
        store_modes(0, step, both[:XROWS] + both[XPAD : XPAD + XROWS] + more[:XROWS])

    for c, (start, stop) in enumerate(LOADS):
        loads[c][0].wait()
        loads[c][1].wait()
        if c == 0:
            by_name["xf"].wait()
            gradient_values(0)

        for step in range(max(start // PAIR, 1), stop // PAIR):
            gradient_modes(step - 1)
            gradient_values(step)

    gradient_modes(ROWS // PAIR - 1)

    def send_rows(t):
        out1[t, 0, BLOCK - 1] = jnp.zeros((8, LANES), F32)
        out1[t, 1, EDGE:BLOCK] = jnp.zeros((BLOCK - EDGE, 8, LANES), F32)
        for half, ks in enumerate((range(FIRST), range(FIRST, HALF))):
            for first in range(ks.start, ks.stop, 2):
                group = range(first, min(first + 2, ks.stop))
                columns = []
                for k in group:
                    real = field_x[t, pl.ds(k, ROWS, stride=XROWS), :]
                    imag = field_x[t, pl.ds(HALF + k, ROWS, stride=XROWS), :]
                    columns.append(jnp.concatenate([real, imag], axis=0))
                both = product(yf[...], stacked(jnp.concatenate(columns, axis=1)))
                for k in group:
                    modes = both[:, (k - first) * LANES : (k - first + 1) * LANES]
                    for d in range(PENCILS):
                        x = d // CORES
                        place = x * FIRST + k if k < FIRST else CHIPS * FIRST + x * REST + k - FIRST
                        out1[t, d % CORES, place] = modes[8 * d : 8 * d + 8]
                    out1[t, 0, EDGE + k // 4, 2 * (k % 4) : 2 * (k % 4) + 2] = modes[64:66]
            pair_copy(t, half).start()

    def pair_copy(t, half):
        tiles = pl.ds(0, CHIPS * FIRST) if half == 0 else pl.ds(CHIPS * FIRST, BLOCK - CHIPS * FIRST)
        return to_pencil(
            out1.at[t, 1 - core, tiles], pair_in.at[t, tiles], psend.at[t], precv.at[t, half], other
        )

    halves = (first_tiles, rest_tiles)
    spans = (pl.ds(0, FIRST), pl.ds(FIRST, REST))

    def x_copy(t, half, to, source):
        return to_pencil(
            sum1.at[t, halves[half](to)], in1.at[t, source, spans[half]], send1.at[t, half], recv1.at[t, source, half],
            to * CORES + core,
        )

    def send_sums(t):
        for half in range(2):
            pair_copy(t, half).wait_recv()
            for j in (2, 1, 3, 0):
                x = (chip + j) % CHIPS
                tiles = halves[half](x)
                sum1[t, tiles] = out1[t, core, tiles] + pair_in[t, tiles]
                if j:
                    x_copy(t, half, x, chip).start()
        sum1[t, EDGE:BLOCK] = out1[t, core, EDGE:BLOCK] + pair_in[t, EDGE:BLOCK]

        @pl.when((core == 0) & (chip != 0))
        def _():
            to_pencil(
                sum1.at[t, pl.ds(EDGE, BLOCK - EDGE)], edge_in.at[t, chip], esend.at[t], erecv.at[t, chip], 0
            ).start()

    by_name["yf"].wait()
    pl.semaphore_wait(barrier, PENCILS - 1 + SLABS - 1)
    send_rows(0)
    send_sums(0)

    @pl.loop(1, PENCILS)
    def _(j):
        d = (pencil + j) % PENCILS
        to_pencil(weight_hbm.at[pl.ds(2 * d, 2)], weights.at[pl.ds(4 * pencil, 2)], wsend, wrecv, d).start()

        @pl.when(d != 0)
        def _():
            to_pencil(
                weight_hbm.at[pl.ds(31 - 2 * d, 2)], weights.at[pl.ds(4 * pencil + 2, 2)], wsend, wrecv, d
            ).start()

        @pl.when(d == 0)
        def _():
            to_pencil(weight_hbm.at[31], weights.at[4 * pencil + 2], wsend, wrecv, d).start()
            to_pencil(weight_hbm.at[16], weights.at[4 * pencil + 3], wsend, wrecv, d).start()

    for q in range(4):
        pltpu.make_async_copy(weight_hbm.at[y_index(pencil, q)], weights.at[4 * pencil + q], own_sem.at[q]).start()

    for c, (start, stop) in enumerate(LOADS):
        loads[c][2].wait()

        @pl.loop(start // PAIR, stop // PAIR, unroll=True)
        def _(step):
            both = product_t(xf[...], act[pl.ds(step * PAIR, PAIR)].reshape(PAIR * LANES, GRID))
            store_modes(1, step, both[:XROWS] + both[XPAD : XPAD + XROWS])

    send_rows(1)
    lane = lax.broadcasted_iota(jnp.int32, (LANES, LANES), 1) // CHAN
    row = lax.broadcasted_iota(jnp.int32, (LANES, LANES), 0) // CHAN

    def send_tiles(t):
        for half, ks in enumerate((range(FIRST), range(FIRST, HALF))):
            total = sum1[t, halves[half](chip)]
            for j in range(1, CHIPS):
                x = (chip + j) % CHIPS
                x_copy(t, half, x, x).wait_recv()
                total = total + in1[t, x, spans[half]]
            for k in ks:
                if k < 16:
                    out2[t, k] = total[k - ks.start]
                if k > 0:
                    out2[t, MODES - k] = total[k - ks.start]

        @pl.when(pencil == 0)
        def _():
            edge = sum1[t, EDGE:BLOCK]
            for x in range(1, CHIPS):
                to_pencil(
                    sum1.at[t, pl.ds(EDGE, BLOCK - EDGE)], edge_in.at[t, x], esend.at[t], erecv.at[t, x], 0
                ).wait_recv()
                edge = edge + edge_in[t, x]
            for k in range(1, HALF):
                r = 2 * (k % 4)
                out2[t, MODES - k, 3:4] = edge[k // 4, r : r + 1]
                out2[t, MODES - k, 7:8] = edge[k // 4, r + 1 : r + 2]

        for d in slab_peers:
            to_slab(out2.at[t, d], in2.at[t, slab], send2.at[t], recv2.at[t], d).start()

        in2[t, slab] = out2[t, slab]

    send_tiles(0)
    send_sums(1)

    sums_acc[...] = jnp.zeros_like(sums_acc)

    @pl.loop(0, ROWS, step=4, unroll=True)
    def _(first):
        left, right = [], []
        for r in range(4):
            left.append(jnp.concatenate([g_high[first + r], g_low[first + r]], axis=0))
            right.append(act[first + r])
        sums_acc[...] += product_t(jnp.concatenate(left, axis=1), jnp.concatenate(right, axis=1))

    full = jnp.where(lane == row, sums_acc[:LANES] + sums_acc[LANES:], 0.0)
    full = jnp.sum(full.reshape(PLANES, CHAN, LANES), axis=0)
    for shift in (CHAN, 2 * CHAN, 4 * CHAN):
        full = full + pltpu.roll(full, shift, 1)
    o_row = lax.broadcasted_iota(jnp.int32, (CHAN, LANES), 0) % 8
    o_lane = lax.broadcasted_iota(jnp.int32, (CHAN, LANES), 1) // CHAN
    full = jnp.where(o_row == o_lane, full, 0.0).reshape(2, 8, LANES)
    full = jnp.sum(full, axis=1, keepdims=True)
    place = lax.broadcasted_iota(jnp.int32, (8, LANES), 0)
    sums_mine[...] = jnp.where(place == 0, full[0], jnp.where(place == 1, full[1], 0.0))

    @pl.loop(1, PENCILS)
    def _(j):
        d = (pencil + j) % PENCILS
        to_pencil(sums_mine, sums_a.at[pencil], asend, arecv.at[pencil], d).start()

    for name in TABLE_NAMES[2:]:
        by_name[name].wait()

    mode_tiles = (MODE_ROWS // 8, 8, LANES)
    place = lax.broadcasted_iota(jnp.int32, mode_tiles, 1)
    first_part = place % 2 == 0
    first_half = place % 4 < 2

    def z_product(table, value):
        high, low = split(value)
        both = product(table[0], jnp.concatenate([high, low], axis=1))
        return both[:, :LANES] + both[:, LANES:] + product(table[1], high)

    def modes_of(t, expand):
        most = pl.ds(0, SLABS - 1)
        to_slab(out2.at[t, most], in2.at[t, most], send2.at[t], recv2.at[t], slab).wait_recv()
        found = z_product(zf, in2[t].reshape(256, LANES)).reshape(mode_tiles)
        found = found * tw[0] + parts_swapped(found) * tw[1]
        high, low = split(found.reshape(MODE_ROWS, LANES))
        wide = product(jnp.concatenate([high, low], axis=1), expand)
        return jnp.where(first_half, wide[:, :LANES].reshape(mode_tiles), wide[:, LANES:].reshape(mode_tiles))

    def both_parts(tile):
        swapped = parts_swapped(tile)
        return jnp.where(first_part, tile, swapped), jnp.where(first_part, swapped, tile)

    to_pencil(
        weight_hbm.at[pl.ds(0, 28)], weights.at[pl.ds(0, 28)], wsend, wrecv, pencil
    ).wait_recv()
    for q in range(4):
        pltpu.make_async_copy(weight_hbm.at[y_index(pencil, q)], weights.at[4 * pencil + q], own_sem.at[q]).wait()
    weight_parts[0], weight_parts[1] = both_parts(weights[...].reshape(mode_tiles))

    lower = modes_of(0, eo[...])
    swapped = parts_swapped(lower)
    turned = jnp.where(first_part, swapped, -swapped)
    low_modes[0] = lower
    low_modes[1] = turned
    high, low = split((weight_parts[0] * lower + weight_parts[1] * turned).reshape(MODE_ROWS, LANES))
    back = product(jnp.concatenate([high, low], axis=1), es[...]).reshape(mode_tiles)
    back = back * tw[0] - parts_swapped(back) * tw[1]
    out3[...] = z_product(zi, back.reshape(MODE_ROWS, LANES)).reshape(SLABS, 8, LANES)

    for d in slab_peers:
        to_slab(out3.at[d], in3.at[slab], send3, recv3, d).start()

    in3[slab] = out3[slab]

    send_tiles(1)

    pick = jnp.where(
        lax.broadcasted_iota(jnp.int32, (LANES, CHAN), 0) % CHAN == lax.broadcasted_iota(jnp.int32, (LANES, CHAN), 1),
        1.0,
        0.0,
    )
    by_name["local"].wait()
    mixed = exact_product(pick, local_ref[...], ((1,), (1,)))
    mixed = exact_product(mixed, pick, ((1,), (1,)))
    mix_high, mix_low = split(jnp.where(lane == row, mixed, 0.0))
    mix_rows = jnp.concatenate([mix_high, mix_high], axis=1)
    mix_more = jnp.concatenate([mix_low, jnp.zeros_like(mix_low)], axis=1)
    mix[...] = jnp.concatenate([mix_rows, mix_more], axis=0)

    @pl.loop(0, ROWS, unroll=4)
    def _(y):
        both = product(mix[...], jnp.concatenate([g_high[y], g_low[y]], axis=0))
        local_part[y] = both[:LANES] + both[LANES:]


    sums_a[pencil] = sums_mine[...]
    for j in range(1, PENCILS):
        d = (pencil + j) % PENCILS
        to_pencil(sums_mine, sums_a.at[d], asend, arecv.at[d], d).wait_recv()
    total = jnp.zeros((8, LANES), F32)
    for d in range(PENCILS):
        total = total + sums_a[d]
    sums_y[my_y] = total
    for j in range(1, 4):
        to_slab(sums_y.at[my_y], sums_y.at[my_y], ysend, yrecv, my_z * 4 + (my_y + j) % 4).start()

    def back_copy(half, p, to, sem):
        return to_pencil(out4.at[spans[half]], in4.at[p, spans[half]], sem, recv4.at[p, half], to)

    to_slab(out3.at[pl.ds(0, SLABS - 1)], in3.at[pl.ds(0, SLABS - 1)], send3, recv3, slab).wait_recv()
    for half, ks in enumerate((range(FIRST), range(FIRST, HALF))):
        for k in ks:
            out4[k] = in3[k] + in3[MODES - k] if 0 < k < 16 else in3[k]

        @pl.when(pencil == 0)
        def _():
            for k in ks:
                for part in range(2):
                    r = 3 + 4 * part
                    if k > 0:
                        edge4[2 * k + part : 2 * k + part + 1] = in3[MODES - k, r : r + 1]
                        out4[k, r : r + 1] = in3[k, r : r + 1] if k < 16 else jnp.zeros((1, LANES), F32)

        for j in (2, 1, 3):
            x = (chip + j) % CHIPS
            back_copy(half, pencil, x * CORES + core, send4.at[half]).start()
        back_copy(half, pencil, other, send4.at[2]).start()

    @pl.when(pencil == 0)
    def _():
        edge4[0:2] = jnp.zeros((2, LANES), F32)
        edge4[34:40] = jnp.zeros((6, LANES), F32)

        @pl.loop(1, PENCILS)
        def _(d):
            to_pencil(edge4, edge4, xsend, xrecv, d).start()

    in4[pencil] = out4[...]

    upper = modes_of(1, ei[...])
    real, imag = both_parts(upper)
    grads[...] = (low_modes[0] * real + low_modes[1] * imag).reshape(MODES, 16, LANES)

    @pl.loop(1, PENCILS)
    def _(j):
        d = (pencil + j) % PENCILS
        to_pencil(grads.at[pl.ds(4 * d, 2)], grad_hbm.at[pl.ds(2 * pencil, 2)], gsend, grecv, d).start()

        @pl.when(pencil != 0)
        def _():
            to_pencil(
                grads.at[pl.ds(4 * d + 2, 2)], grad_hbm.at[pl.ds(31 - 2 * pencil, 2)], gsend, grecv, d
            ).start()

        @pl.when(pencil == 0)
        def _():
            to_pencil(grads.at[4 * d + 2], grad_hbm.at[31], gsend, grecv, d).start()
            to_pencil(grads.at[4 * d + 3], grad_hbm.at[16], gsend, grecv, d).start()

    for q in range(4):
        pltpu.make_async_copy(grads.at[4 * pencil + q], grad_hbm.at[y_index(pencil, q)], own_sem.at[4 + q]).start()

    to_slab(sums_y.at[pl.ds(0, 3)], sums_y.at[pl.ds(0, 3)], ysend, yrecv, slab).wait_recv()
    total = sums_y[0]
    for j in range(1, 4):
        total = total + sums_y[j]
    sums_z[my_z] = total
    for j in range(1, 8):
        to_slab(sums_z.at[my_z], sums_z.at[my_z], zsend, zrecv, (my_z + j) % 8 * 4 + my_y).start()

    for half in range(2):
        for j in (1, 3, 2):
            d = (chip + j) % CHIPS * CORES + core
            back_copy(half, d, d, send4.at[half]).wait_recv()
            to_pencil(
                in4.at[d, spans[half]], in4.at[d, spans[half]], fsend.at[half], recv4.at[d, half], other
            ).start()

    @pl.when(pencil != 0)
    def _():
        to_pencil(edge4, edge4, xsend, xrecv, 0).wait_recv()

    spread_y[pl.ds(2 * HALF * ROWS, (XROWS - 2 * HALF) * ROWS), :] = jnp.zeros(((XROWS - 2 * HALF) * ROWS, LANES), F32)
    for half, ks in enumerate((range(FIRST), range(FIRST, HALF))):
        for x in range(CHIPS):
            back_copy(half, x * CORES + 1 - core, other, send4.at[2]).wait_recv()
        for first in range(ks.start, ks.stop, 2):
            group = range(first, min(first + 2, ks.stop))
            columns = [jnp.concatenate([in4[p, k] for p in range(PENCILS)], axis=0) for k in group]
            both = product(yi[...], stacked(jnp.concatenate(columns, axis=1)))
            for k in group:
                field = both[:, (k - first) * LANES : (k - first + 1) * LANES]
                edge_real, edge_imag = edge4[2 * k : 2 * k + 1], edge4[2 * k + 1 : 2 * k + 2]
                spread_y[k * ROWS : (k + 1) * ROWS] = field[:ROWS] + ye[0] * edge_real - ye[1] * edge_imag
                spread_y[(HALF + k) * ROWS : (HALF + k + 1) * ROWS] = (
                    field[ROWS:] + ye[0] * edge_imag + ye[1] * edge_real
                )

    to_slab(sums_z.at[pl.ds(0, 7)], sums_z.at[pl.ds(0, 7)], zsend, zrecv, slab).wait_recv()
    total = sums_z[0]
    for j in range(1, 8):
        total = total + sums_z[j]
    sums_all[...] = total * float(GRID) ** -1.5
    stores = [pltpu.make_async_copy(sums_all, sum_hbm, store_sem.at[chunks])]
    stores[0].start()

    for c in range(chunks):

        columns = []
        for r in range(CHUNK):
            value = spread_y[pl.ds(c * CHUNK + r, XROWS, stride=ROWS), :]
            high = value.astype(BF16).astype(F32)
            column = jnp.concatenate([high, value - high, high, jnp.zeros((8, LANES), F32)], axis=0)
            columns.append(column.T.astype(BF16))
        fields = product(jnp.concatenate(columns, axis=0), xi[...])
        for r in range(CHUNK):
            y = c * CHUNK + r
            result[y] = (local_part[y] + fields[r * LANES : (r + 1) * LANES]).astype(BF16)

        rows = pl.ds(c * CHUNK, CHUNK)
        stores.append(pltpu.make_async_copy(result.at[rows], result_hbm.at[rows], store_sem.at[c]))
        stores[-1].start()

    to_pencil(weights.at[pl.ds(0, 28)], weights.at[pl.ds(0, 28)], wsend, wrecv, pencil).wait_send()
    for t in range(2):
        to_pencil(out1.at[t, 1 - core], pair_in.at[t], psend.at[t], precv.at[t, 0], other).wait_send()
        for half in range(2):
            some = in1.at[t, pl.ds(0, 3), spans[half]]
            to_pencil(some, some, send1.at[t, half], recv1.at[t, 0, half], other).wait_send()
        most = pl.ds(0, SLABS - 1)
        to_slab(out2.at[t, most], in2.at[t, most], send2.at[t], recv2.at[t], slab).wait_send()

        @pl.when((core == 0) & (chip != 0))
        def _():
            to_pencil(
                sum1.at[t, pl.ds(EDGE, BLOCK - EDGE)], edge_in.at[t, chip], esend.at[t], erecv.at[t, chip], 0
            ).wait_send()

    to_pencil(sums_a.at[pl.ds(0, 7)], sums_a.at[pl.ds(0, 7)], asend, arecv.at[0], pencil).wait_send()
    to_slab(sums_y.at[pl.ds(0, 3)], sums_y.at[pl.ds(0, 3)], ysend, yrecv, slab).wait_send()
    to_slab(sums_z.at[pl.ds(0, 7)], sums_z.at[pl.ds(0, 7)], zsend, zrecv, slab).wait_send()
    to_slab(out3.at[pl.ds(0, 31)], in3.at[pl.ds(0, 31)], send3, recv3, slab).wait_send()
    for half in range(2):
        some = in4.at[pl.ds(0, 3), spans[half]]
        to_pencil(some, some, send4.at[half], recv4.at[0, half], other).wait_send()
        to_pencil(some, some, fsend.at[half], recv4.at[0, half], other).wait_send()
    to_pencil(out4, in4.at[pencil], send4.at[2], recv4.at[pencil, 0], other).wait_send()

    @pl.when(pencil == 0)
    def _():
        for d in range(1, PENCILS):
            to_pencil(edge4, edge4, xsend, xrecv, d).wait_send()

    to_pencil(grads.at[pl.ds(0, 28)], grad_hbm.at[pl.ds(0, 28)], gsend, grecv, pencil).wait()
    for q in range(4):
        pltpu.make_async_copy(grads.at[4 * pencil + q], grad_hbm.at[y_index(pencil, q)], own_sem.at[4 + q]).wait()
    for store in stores:
        store.wait()


def last_kernel(
    result_hbm, grad_in, sum_hbm,
    out_hbm, local_hbm, grad_out,
    result, grad, sum_ref, local_ref, load_sem, store_sem,
):
    rows = [pl.ds(c * (ROWS // PARTS), ROWS // PARTS) for c in range(PARTS)]
    loads = [pltpu.make_async_copy(result_hbm.at[r], result.at[r], load_sem.at[c]) for c, r in enumerate(rows)]
    stores = [pltpu.make_async_copy(result.at[r], out_hbm.at[r], store_sem.at[c]) for c, r in enumerate(rows)]
    loads.append(pltpu.make_async_copy(grad_in, grad, load_sem.at[PARTS]))
    stores.append(pltpu.make_async_copy(grad, grad_out, store_sem.at[PARTS]))
    load_sum = pltpu.make_async_copy(sum_hbm, sum_ref, load_sem.at[PARTS + 1])
    load_sum.start()
    for load in loads:
        load.start()

    o_row = lax.broadcasted_iota(jnp.int32, (CHAN, LANES), 0)
    o_lane = lax.broadcasted_iota(jnp.int32, (CHAN, LANES), 1)
    load_sum.wait()
    total = jnp.where(o_row < 8, sum_ref[0:1], sum_ref[1:2])
    total = jnp.where(o_row % 8 == o_lane // CHAN, total, 0.0)
    pick = jnp.where(
        lax.broadcasted_iota(jnp.int32, (LANES, CHAN), 0) % CHAN == lax.broadcasted_iota(jnp.int32, (LANES, CHAN), 1),
        1.0,
        0.0,
    )
    local_ref[...] = exact_product(total, pick, ((1,), (0,)))
    store_local = pltpu.make_async_copy(local_ref, local_hbm, store_sem.at[PARTS + 1])
    store_local.start()
    for load, store in zip(loads, stores):
        load.wait()
        store.start()
    for store in stores:
        store.wait()
    store_local.wait()


def on_device(activation, preact, cotangent, local_weight, spectral_weight):
    made = tables()
    fields = [a.reshape(ROWS, LANES, GRID) for a in (activation, preact, cotangent)]
    weight = spectral_weight[0].reshape(MODES, 4, 2, 2, LANES).transpose(0, 1, 3, 2, 4).reshape(MODES, 16, LANES)
    any_space = pl.BlockSpec(memory_space=pl.ANY)
    dma = pltpu.SemaphoreType.DMA
    field = pltpu.VMEM((ROWS, LANES, GRID), BF16)
    wide_field = pltpu.VMEM((ROWS, LANES, GRID), F32)
    tile = (8, LANES)
    result, grad, total = pl.pallas_call(
        modes_kernel,
        out_shape=(
            jax.ShapeDtypeStruct((ROWS, LANES, GRID), BF16),
            jax.ShapeDtypeStruct((MODES, 16, LANES), F32),
            jax.ShapeDtypeStruct(tile, F32),
        ),
        in_specs=[any_space] * (5 + len(TABLE_NAMES)),
        out_specs=(any_space, any_space, any_space),
        scratch_shapes=[
            field, field, field, field, field, wide_field, field,
            pltpu.VMEM((2 * XPAD, GRID), BF16),
            pltpu.VMEM((80, 192), BF16),
            pltpu.VMEM((2, MODE_ROWS, 256), BF16),
            pltpu.VMEM((2, 256, MODE_ROWS), BF16),
            pltpu.VMEM((2, MODE_ROWS // 8, 8, LANES), F32),
            pltpu.VMEM((256, 256), BF16),
            pltpu.VMEM((256, 256), BF16),
            pltpu.VMEM((256, LANES), BF16),
            pltpu.VMEM((64, 192), BF16),
            pltpu.VMEM((2, ROWS, LANES), F32),
            pltpu.VMEM((128, GRID), BF16),
            pltpu.VMEM((2, ROWS * XROWS, LANES), F32),
            pltpu.VMEM((ROWS * XROWS, LANES), F32),
            pltpu.VMEM((2, CORES, BLOCK) + tile, F32),
            pltpu.VMEM((2, BLOCK) + tile, F32),
            pltpu.VMEM((2, BLOCK) + tile, F32),
            pltpu.VMEM((2, CHIPS, HALF) + tile, F32),
            pltpu.VMEM((2, CHIPS, BLOCK - EDGE) + tile, F32),
            pltpu.VMEM((2, SLABS) + tile, F32),
            pltpu.VMEM((2, SLABS) + tile, F32),
            pltpu.VMEM((MODES, 16, LANES), F32),
            pltpu.VMEM((2, MODE_ROWS // 8, 8, LANES), F32),
            pltpu.VMEM((2, MODE_ROWS // 8, 8, LANES), F32),
            pltpu.VMEM((SLABS,) + tile, F32),
            pltpu.VMEM((SLABS,) + tile, F32),
            pltpu.VMEM((HALF,) + tile, F32),
            pltpu.VMEM((PENCILS, HALF) + tile, F32),
            pltpu.VMEM((XROWS, LANES), F32),
            pltpu.VMEM((MODES, 16, LANES), F32),
            pltpu.VMEM((2 * LANES, LANES), F32),
            pltpu.VMEM((PENCILS,) + tile, F32),
            pltpu.VMEM((4,) + tile, F32),
            pltpu.VMEM((8,) + tile, F32),
            pltpu.VMEM(tile, F32),
            pltpu.VMEM(tile, F32),
            pltpu.VMEM((CHAN, CHAN), F32),
            pltpu.VMEM((2 * LANES, 2 * LANES), BF16),
            dma((len(TABLE_NAMES) + 1,)), dma((3, len(LOADS))), dma((ROWS // CHUNK + 1,)), dma((8,)),
            dma((2,)), dma((2, 2)), dma((2, 2)), dma((2, CHIPS, 2)), dma((2,)), dma((2, CHIPS)),
            dma((2,)), dma((2,)), dma, dma,
            dma, dma, dma((3,)), dma((PENCILS, 2)), dma((2,)), dma, dma, dma, dma,
            dma, dma((PENCILS,)), dma, dma, dma, dma,
        ],
        compiler_params=pltpu.CompilerParams(
            collective_id=0, has_side_effects=True, vmem_limit_bytes=62 * 1024 * 1024
        ),
        cost_estimate=pl.CostEstimate(flops=3_000_000_000, bytes_accessed=11_000_000, transcendentals=2_000_000),
        name="modes",
    )(*fields, weight, local_weight, *(jnp.asarray(made[name]) for name in TABLE_NAMES))
    out, grad_local, grad_spectral = pl.pallas_call(
        last_kernel,
        out_shape=(
            jax.ShapeDtypeStruct((ROWS, LANES, GRID), BF16),
            jax.ShapeDtypeStruct((CHAN, CHAN), F32),
            jax.ShapeDtypeStruct((MODES, 16, LANES), F32),
        ),
        in_specs=[any_space, any_space, any_space],
        out_specs=(any_space, any_space, any_space),
        scratch_shapes=[
            field,
            pltpu.VMEM((MODES, 16, LANES), F32),
            pltpu.VMEM(tile, F32),
            pltpu.VMEM((CHAN, CHAN), F32),
            dma((PARTS + 2,)), dma((PARTS + 2,)),
        ],
        compiler_params=pltpu.CompilerParams(vmem_limit_bytes=62 * 1024 * 1024),
        cost_estimate=pl.CostEstimate(flops=100_000, bytes_accessed=5_000_000, transcendentals=0),
        name="last",
    )(result, grad, total)
    grad_spectral = grad_spectral.reshape(MODES, 4, 2, 2, LANES).transpose(0, 1, 3, 2, 4).reshape(spectral_weight.shape)
    return out.reshape(activation.shape), grad_local, grad_spectral


def solution(mesh):
    field = P("pencil", "slab", None, None)
    modes = P("slab", None, "pencil", None, None)
    return jax.shard_map(
        on_device,
        mesh=mesh,
        in_specs=(field, field, field, P(), modes),
        out_specs=(field, P(), modes),
        check_vma=False,
    )
```

```python
import functools

import jax
import jax.numpy as jnp
import ml_dtypes
import numpy as np
from jax import lax
from jax.experimental import pallas as pl
from jax.experimental.pallas import tpu as pltpu
from jax.sharding import PartitionSpec as P

GRID = 256
CHAN = 16
MODES = 32
SLABS = 32
PENCILS = 8
ROWS = GRID // PENCILS
PLANES = GRID // SLABS
LANES = PLANES * CHAN
HALF = MODES // 2 + 1
XROWS = 40
XPAD = 48
CORES = 2
CHIPS = PENCILS // CORES
FIRST = 9
REST = HALF - FIRST
EDGE = CHIPS * HALF
BLOCK = EDGE + XROWS // 8
PARTS = 8
MODE_ROWS = 512
CHUNK = 8
LOADS = ((0, 4), (4, 8), (8, 16), (16, 24), (24, 32))
PAIR = 2
F32 = jnp.float32
BF16 = jnp.bfloat16


def kept(j):
    return np.where(j < MODES // 2, j, j - MODES)


def y_set(p):
    if p == 0:
        return np.array([0, 1, -1, -16])
    return np.array([2 * p, 2 * p + 1, -2 * p - 1, -2 * p])


def pieces(table):
    high = table.astype(np.float32).astype(ml_dtypes.bfloat16)
    low = (table - high.astype(np.float64)).astype(np.float32).astype(ml_dtypes.bfloat16)
    return high, low


def turn(freq, position):
    angle = 2.0 * np.pi * ((freq * position) % GRID) / GRID
    return np.cos(angle), np.sin(angle)


@functools.cache
def tables():
    made = {}
    cells = np.arange(GRID)

    cosine, sine = turn(np.arange(HALF)[:, None], cells[None, :])
    forward_x = np.zeros((XPAD, GRID))
    forward_x[:HALF], forward_x[HALF : 2 * HALF] = cosine, -sine
    high, low = pieces(forward_x[:XROWS].T)
    rest = np.zeros((GRID, LANES - 2 * XROWS), high.dtype)
    for_high = np.concatenate([high, low, rest], axis=1)
    for_low = np.concatenate([high, np.zeros_like(low), rest], axis=1)
    made["xf"] = np.concatenate([for_high, for_low], axis=0)
    high, low = pieces(forward_x[:XROWS])
    made["xi"] = np.concatenate([high, high, low, np.zeros((8, GRID), high.dtype)], axis=0)

    forward_y = np.zeros((PENCILS, 80, 2, ROWS))
    inverse_y = np.zeros((PENCILS, 2, ROWS, PENCILS, 2, 4))
    extra_y = np.zeros((PENCILS, 2, ROWS, LANES))
    for p in range(PENCILS):
        rows = p * ROWS + np.arange(ROWS)
        for d in range(PENCILS):
            cosine, sine = turn(y_set(d)[:, None], rows[None, :])
            forward_y[p, 8 * d : 8 * d + 4, 0], forward_y[p, 8 * d : 8 * d + 4, 1] = cosine, sine
            forward_y[p, 8 * d + 4 : 8 * d + 8, 0], forward_y[p, 8 * d + 4 : 8 * d + 8, 1] = -sine, cosine
            inverse_y[p, 0, :, d, 0], inverse_y[p, 0, :, d, 1] = cosine.T, -sine.T
            inverse_y[p, 1, :, d, 0], inverse_y[p, 1, :, d, 1] = sine.T, cosine.T
        cosine, sine = turn(16, rows)
        forward_y[p, 64, 0], forward_y[p, 64, 1] = cosine, sine
        forward_y[p, 65, 0], forward_y[p, 65, 1] = -sine, cosine
        extra_y[p, 0], extra_y[p, 1] = cosine[:, None], sine[:, None]
    high, low = pieces(forward_y.reshape(PENCILS, 80, 2 * ROWS))
    made["yf"] = np.concatenate([high, high, low], axis=2)
    high, low = pieces(inverse_y.reshape(PENCILS, 2 * ROWS, 64))
    made["yi"] = np.concatenate([high, high, low], axis=2)
    made["ye"] = extra_y.astype(np.float32)

    z_freq = kept(np.arange(MODES)).reshape(8, 4)
    slab = np.arange(SLABS)
    cosine, sine = turn(z_freq[:, :, None], 8 * slab[None, None, :])
    cosine, sine = cosine[:, :, None, :], sine[:, :, None, :]
    forward_z = np.zeros((8, 4, 4, 2, 2, SLABS, 2, 4))
    for q in range(4):
        forward_z[:, q, :, :, 0, :, 0, q], forward_z[:, q, :, :, 0, :, 1, q] = cosine, sine
        forward_z[:, q, :, :, 1, :, 0, q], forward_z[:, q, :, :, 1, :, 1, q] = -sine, cosine
    forward_z = forward_z.reshape(MODE_ROWS, SLABS, 8)
    kinds = [forward_z]
    for order in ([3, 2, 1, 0], [0, 2, 1, 3]):
        mirrored = np.zeros_like(forward_z)
        for q in range(4):
            mirrored[:, :, order[q]] = forward_z[:, :, q]
            mirrored[:, :, 4 + order[q]] = -forward_z[:, :, 4 + q]
        kinds.append(mirrored)
    kinds = np.stack(kinds).reshape(3, MODE_ROWS, 256)
    made["zf"] = np.stack(pieces(kinds), axis=1)
    made["zi"] = np.stack(pieces(kinds.transpose(0, 2, 1)), axis=1)
    cosine, sine = turn(z_freq[:, :, None], np.arange(PLANES)[None, None, :])
    spread = np.zeros((2, 8, 4, 4, 2, 2, PLANES, CHAN))
    spread[0] = cosine[:, None, :, None, None, :, None]
    spread[1, :, :, :, :, 0] = sine[:, None, :, None, :, None]
    spread[1, :, :, :, :, 1] = -sine[:, None, :, None, :, None]
    made["tw"] = spread.reshape(2, MODE_ROWS // 8, 8, LANES).astype(np.float32)

    same = np.eye(CHAN)
    of_output = np.broadcast_to(same[None, :, :, None], (PLANES, CHAN, CHAN, CHAN)).reshape(LANES, 256)
    of_input = np.broadcast_to(same[None, :, None, :], (PLANES, CHAN, CHAN, CHAN)).reshape(LANES, 256)
    made["eo"] = (np.concatenate([of_output, of_output]) * float(GRID) ** -3).astype(ml_dtypes.bfloat16)
    made["ei"] = np.concatenate([of_input, of_input]).astype(ml_dtypes.bfloat16)
    made["es"] = np.concatenate([of_input.T[:LANES]] * 2).astype(ml_dtypes.bfloat16)
    return made


TABLE_NAMES = ("xf", "yf", "zf", "zi", "tw", "eo", "ei", "es", "yi", "ye", "xi")


def product(a, b):
    return lax.dot_general(a, b, (((1,), (0,)), ((), ())), preferred_element_type=F32)


def product_t(a, b):
    return lax.dot_general(a, b, (((1,), (1,)), ((), ())), preferred_element_type=F32)


def exact_product(a, b, dims):
    return lax.dot_general(a, b, (dims, ((), ())), precision=lax.Precision.HIGHEST, preferred_element_type=F32)


def split(value):
    high = value.astype(BF16)
    return high, (value - high.astype(F32)).astype(BF16)


def stacked(value):
    high, low = split(value)
    return jnp.concatenate([high, low, high], axis=0)


def gelu_slope(value):
    normal_cdf = 0.5 * (1.0 + lax.erf(value * 0.7071067811865476))
    density = jnp.exp(-0.5 * value * value) * 0.3989422804014327
    return normal_cdf + value * density


def parts_swapped(tile):
    even = lax.broadcasted_iota(jnp.int32, tile.shape, 1) % 2 == 0
    return jnp.where(even, pltpu.roll(tile, 7, 1), pltpu.roll(tile, 1, 1))


def to_pencil(src, dst, send, recv, d):
    return pltpu.make_async_remote_copy(
        src_ref=src,
        dst_ref=dst,
        send_sem=send,
        recv_sem=recv,
        device_id={"pencil": d},
        device_id_type=pl.DeviceIdType.MESH,
    )


def to_slab(src, dst, send, recv, d):
    return pltpu.make_async_remote_copy(
        src_ref=src,
        dst_ref=dst,
        send_sem=send,
        recv_sem=recv,
        device_id={"slab": d},
        device_id_type=pl.DeviceIdType.MESH,
    )


def first_tiles(x):
    return pl.ds(x * FIRST, FIRST)


def rest_tiles(x):
    return pl.ds(CHIPS * FIRST + x * REST, REST)


def y_index(p, q):
    if q < 2:
        return 2 * p + q
    if q == 2:
        return 31 - 2 * p
    return jnp.where(p == 0, 16, 32 - 2 * p)


def modes_kernel(
    act_hbm, pre_hbm, cot_hbm, weight_hbm, local_hbm,
    xf_hbm, yf_hbm, zf_hbm, zi_hbm, tw_hbm, eo_hbm, ei_hbm, es_hbm, yi_hbm, ye_hbm, xi_hbm,
    result_hbm, grad_hbm, sum_hbm,
    act, pre, cot, g_high, g_low, local_part, result,
    xf, yf, zf, zi, tw, eo, ei, es, yi, ye, xi,
    field_x, spread_y,
    out1, pair_in, sum1, in1, edge_in, out2, in2,
    weights, weight_parts, low_modes, out3, in3, out4, in4, edge4, grads,
    sums_acc, sums_a, sums_y, sums_z, sums_mine, sums_all, local_ref, mix,
    table_sem, load_sem, store_sem, own_sem,
    psend, precv, send1, recv1, esend, erecv, send2, recv2, wsend, wrecv,
    send3, recv3, send4, recv4, fsend, xsend, xrecv, gsend, grecv,
    asend, arecv, ysend, yrecv, zsend, zrecv,
):
    slab = lax.axis_index("slab")
    pencil = lax.axis_index("pencil")
    core, chip = pencil % CORES, pencil // CORES
    other = chip * CORES + 1 - core

    my_z, my_y = slab // 4, slab % 4

    slab_peers = [
        (slab // 4 + far_z) % 8 * 4 + (slab + far_y) % 4
        for far_z in (4, 3, 5, 2, 6, 1, 7, 0)
        for far_y in (2, 1, 3, 0)
        if far_z or far_y
    ]

    chunks = ROWS // CHUNK
    loads = []
    for c, (start, stop) in enumerate(LOADS):
        rows = pl.ds(start, stop - start)
        loads.append(
            [
                pltpu.make_async_copy(pre_hbm.at[rows], pre.at[rows], load_sem.at[0, c]),
                pltpu.make_async_copy(cot_hbm.at[rows], cot.at[rows], load_sem.at[1, c]),
                pltpu.make_async_copy(act_hbm.at[rows], act.at[rows], load_sem.at[2, c]),
            ]
        )
    kind = jnp.where(slab < 16, 0, jnp.where(pencil == 0, 2, 1))
    sources = (
        (xf_hbm, xf), (yf_hbm.at[pencil], yf), (zf_hbm.at[kind], zf), (zi_hbm.at[kind], zi), (tw_hbm, tw), (eo_hbm, eo), (ei_hbm, ei), (es_hbm, es),
        (yi_hbm.at[pencil], yi), (ye_hbm.at[pencil], ye), (xi_hbm, xi),
        (local_hbm, local_ref),
    )
    fetch = [pltpu.make_async_copy(a, b, table_sem.at[n]) for n, (a, b) in enumerate(sources)]
    by_name = dict(zip(TABLE_NAMES + ("local",), fetch))
    loads[0][0].start()
    loads[0][1].start()
    by_name["xf"].start()
    for load in loads[1:]:
        load[0].start()
        load[1].start()
    by_name["yf"].start()
    for load in loads:
        load[2].start()
    for name in by_name:
        if name not in ("xf", "yf"):
            by_name[name].start()

    barrier = pltpu.get_barrier_semaphore()

    @pl.loop(1, PENCILS)
    def _(j):
        pl.semaphore_signal(
            barrier, inc=1, device_id={"pencil": (pencil + j) % PENCILS}, device_id_type=pl.DeviceIdType.MESH
        )

    @pl.loop(1, SLABS)
    def _(j):
        pl.semaphore_signal(barrier, inc=1, device_id={"slab": (slab + j) % SLABS}, device_id_type=pl.DeviceIdType.MESH)

    def gradient_values(step):
        for r in range(PAIR):
            y = step * PAIR + r
            for part in range(4):
                rows = pl.ds(part * (LANES // 4), LANES // 4)
                g = cot[y, rows].astype(F32) * gelu_slope(pre[y, rows].astype(F32))
                high, low = split(g)
                g_high[y, rows] = high
                g_low[y, rows] = low

    def store_modes(t, step, modes):
        for r in range(PAIR):
            place = (step * PAIR + r) * XROWS
            place = place if isinstance(place, int) else pl.multiple_of(place, 8)
            turned = modes[r * LANES : (r + 1) * LANES].T
            field_x[t, pl.ds(place, XROWS), :] = turned[:XROWS] + turned[XROWS : 2 * XROWS]

    def gradient_modes(step):
        rows = pl.ds(step * PAIR, PAIR)
        high, low = g_high[rows].reshape(PAIR * LANES, GRID), g_low[rows].reshape(PAIR * LANES, GRID)
        store_modes(0, step, product(jnp.concatenate([high, low], axis=1), xf[...]))

    for c, (start, stop) in enumerate(LOADS):
        loads[c][0].wait()
        loads[c][1].wait()
        if c == 0:
            by_name["xf"].wait()
            gradient_values(0)

        for step in range(max(start // PAIR, 1), stop // PAIR):
            gradient_modes(step - 1)
            gradient_values(step)

    gradient_modes(ROWS // PAIR - 1)

    def send_rows(t):
        out1[t, 0, BLOCK - 1] = jnp.zeros((8, LANES), F32)
        out1[t, 1, EDGE:BLOCK] = jnp.zeros((BLOCK - EDGE, 8, LANES), F32)
        for half, ks in enumerate((range(FIRST), range(FIRST, HALF))):
            for first in range(ks.start, ks.stop, 2):
                group = range(first, min(first + 2, ks.stop))
                columns = []
                for k in group:
                    real = field_x[t, pl.ds(k, ROWS, stride=XROWS), :]
                    imag = field_x[t, pl.ds(HALF + k, ROWS, stride=XROWS), :]
                    columns.append(jnp.concatenate([real, imag], axis=0))
                both = product(yf[...], stacked(jnp.concatenate(columns, axis=1)))
                for k in group:
                    modes = both[:, (k - first) * LANES : (k - first + 1) * LANES]
                    for d in range(PENCILS):
                        x = d // CORES
                        place = x * FIRST + k if k < FIRST else CHIPS * FIRST + x * REST + k - FIRST
                        out1[t, d % CORES, place] = modes[8 * d : 8 * d + 8]
                    out1[t, 0, EDGE + k // 4, 2 * (k % 4) : 2 * (k % 4) + 2] = modes[64:66]
            pair_copy(t, half).start()

    def pair_copy(t, half):
        tiles = pl.ds(0, CHIPS * FIRST) if half == 0 else pl.ds(CHIPS * FIRST, BLOCK - CHIPS * FIRST)
        return to_pencil(
            out1.at[t, 1 - core, tiles], pair_in.at[t, tiles], psend.at[t], precv.at[t, half], other
        )

    halves = (first_tiles, rest_tiles)
    spans = (pl.ds(0, FIRST), pl.ds(FIRST, REST))

    def x_copy(t, half, to, source):
        return to_pencil(
            sum1.at[t, halves[half](to)], in1.at[t, source, spans[half]], send1.at[t, half], recv1.at[t, source, half],
            to * CORES + core,
        )

    def send_sums(t):
        for half in range(2):
            pair_copy(t, half).wait_recv()
            for j in (2, 1, 3, 0):
                x = (chip + j) % CHIPS
                tiles = halves[half](x)
                sum1[t, tiles] = out1[t, core, tiles] + pair_in[t, tiles]
                if j:
                    x_copy(t, half, x, chip).start()
        sum1[t, EDGE:BLOCK] = out1[t, core, EDGE:BLOCK] + pair_in[t, EDGE:BLOCK]

        @pl.when((core == 0) & (chip != 0))
        def _():
            to_pencil(
                sum1.at[t, pl.ds(EDGE, BLOCK - EDGE)], edge_in.at[t, chip], esend.at[t], erecv.at[t, chip], 0
            ).start()

    by_name["yf"].wait()
    pl.semaphore_wait(barrier, PENCILS - 1 + SLABS - 1)
    send_rows(0)
    send_sums(0)

    @pl.loop(1, PENCILS)
    def _(j):
        d = (pencil + j) % PENCILS
        to_pencil(weight_hbm.at[pl.ds(2 * d, 2)], weights.at[pl.ds(4 * pencil, 2)], wsend, wrecv, d).start()

        @pl.when(d != 0)
        def _():
            to_pencil(
                weight_hbm.at[pl.ds(31 - 2 * d, 2)], weights.at[pl.ds(4 * pencil + 2, 2)], wsend, wrecv, d
            ).start()

        @pl.when(d == 0)
        def _():
            to_pencil(weight_hbm.at[31], weights.at[4 * pencil + 2], wsend, wrecv, d).start()
            to_pencil(weight_hbm.at[16], weights.at[4 * pencil + 3], wsend, wrecv, d).start()

    for q in range(4):
        pltpu.make_async_copy(weight_hbm.at[y_index(pencil, q)], weights.at[4 * pencil + q], own_sem.at[q]).start()

    for c, (start, stop) in enumerate(LOADS):
        loads[c][2].wait()

        @pl.loop(start // PAIR, stop // PAIR, unroll=True)
        def _(step):
            store_modes(1, step, product(act[pl.ds(step * PAIR, PAIR)].reshape(PAIR * LANES, GRID), xf[:GRID]))

    send_rows(1)
    lane = lax.broadcasted_iota(jnp.int32, (LANES, LANES), 1) // CHAN
    row = lax.broadcasted_iota(jnp.int32, (LANES, LANES), 0) // CHAN

    def send_tiles(t):
        for half, ks in enumerate((range(FIRST), range(FIRST, HALF))):
            total = sum1[t, halves[half](chip)]
            for j in range(1, CHIPS):
                x = (chip + j) % CHIPS
                x_copy(t, half, x, x).wait_recv()
                total = total + in1[t, x, spans[half]]
            for k in ks:
                if k < 16:
                    out2[t, k] = total[k - ks.start]
                if k > 0:
                    out2[t, MODES - k] = total[k - ks.start]

        @pl.when(pencil == 0)
        def _():
            edge = sum1[t, EDGE:BLOCK]
            for x in range(1, CHIPS):
                to_pencil(
                    sum1.at[t, pl.ds(EDGE, BLOCK - EDGE)], edge_in.at[t, x], esend.at[t], erecv.at[t, x], 0
                ).wait_recv()
                edge = edge + edge_in[t, x]
            for k in range(1, HALF):
                r = 2 * (k % 4)
                out2[t, MODES - k, 3:4] = edge[k // 4, r : r + 1]
                out2[t, MODES - k, 7:8] = edge[k // 4, r + 1 : r + 2]

        for d in slab_peers:
            to_slab(out2.at[t, d], in2.at[t, slab], send2.at[t], recv2.at[t], d).start()

        in2[t, slab] = out2[t, slab]

    send_tiles(0)
    send_sums(1)

    sums_acc[...] = jnp.zeros_like(sums_acc)

    @pl.loop(0, ROWS, step=4, unroll=True)
    def _(first):
        left, right = [], []
        for r in range(4):
            left.append(jnp.concatenate([g_high[first + r], g_low[first + r]], axis=0))
            right.append(act[first + r])
        sums_acc[...] += product_t(jnp.concatenate(left, axis=1), jnp.concatenate(right, axis=1))

    full = jnp.where(lane == row, sums_acc[:LANES] + sums_acc[LANES:], 0.0)
    full = jnp.sum(full.reshape(PLANES, CHAN, LANES), axis=0)
    for shift in (CHAN, 2 * CHAN, 4 * CHAN):
        full = full + pltpu.roll(full, shift, 1)
    o_row = lax.broadcasted_iota(jnp.int32, (CHAN, LANES), 0) % 8
    o_lane = lax.broadcasted_iota(jnp.int32, (CHAN, LANES), 1) // CHAN
    full = jnp.where(o_row == o_lane, full, 0.0).reshape(2, 8, LANES)
    full = jnp.sum(full, axis=1, keepdims=True)
    place = lax.broadcasted_iota(jnp.int32, (8, LANES), 0)
    sums_mine[...] = jnp.where(place == 0, full[0], jnp.where(place == 1, full[1], 0.0))

    @pl.loop(1, PENCILS)
    def _(j):
        d = (pencil + j) % PENCILS
        to_pencil(sums_mine, sums_a.at[pencil], asend, arecv.at[pencil], d).start()

    for name in TABLE_NAMES[2:]:
        by_name[name].wait()

    mode_tiles = (MODE_ROWS // 8, 8, LANES)
    place = lax.broadcasted_iota(jnp.int32, mode_tiles, 1)
    first_part = place % 2 == 0
    first_half = place % 4 < 2

    def z_product(table, value):
        high, low = split(value)
        both = product(table[0], jnp.concatenate([high, low], axis=1))
        return both[:, :LANES] + both[:, LANES:] + product(table[1], high)

    def modes_of(t, expand):
        most = pl.ds(0, SLABS - 1)
        to_slab(out2.at[t, most], in2.at[t, most], send2.at[t], recv2.at[t], slab).wait_recv()
        found = z_product(zf, in2[t].reshape(256, LANES)).reshape(mode_tiles)
        found = found * tw[0] + parts_swapped(found) * tw[1]
        high, low = split(found.reshape(MODE_ROWS, LANES))
        wide = product(jnp.concatenate([high, low], axis=1), expand)
        return jnp.where(first_half, wide[:, :LANES].reshape(mode_tiles), wide[:, LANES:].reshape(mode_tiles))

    def both_parts(tile):
        swapped = parts_swapped(tile)
        return jnp.where(first_part, tile, swapped), jnp.where(first_part, swapped, tile)

    to_pencil(
        weight_hbm.at[pl.ds(0, 28)], weights.at[pl.ds(0, 28)], wsend, wrecv, pencil
    ).wait_recv()
    for q in range(4):
        pltpu.make_async_copy(weight_hbm.at[y_index(pencil, q)], weights.at[4 * pencil + q], own_sem.at[q]).wait()
    weight_parts[0], weight_parts[1] = both_parts(weights[...].reshape(mode_tiles))

    lower = modes_of(0, eo[...])
    swapped = parts_swapped(lower)
    turned = jnp.where(first_part, swapped, -swapped)
    low_modes[0] = lower
    low_modes[1] = turned
    high, low = split((weight_parts[0] * lower + weight_parts[1] * turned).reshape(MODE_ROWS, LANES))
    back = product(jnp.concatenate([high, low], axis=1), es[...]).reshape(mode_tiles)
    back = back * tw[0] - parts_swapped(back) * tw[1]
    out3[...] = z_product(zi, back.reshape(MODE_ROWS, LANES)).reshape(SLABS, 8, LANES)

    for d in slab_peers:
        to_slab(out3.at[d], in3.at[slab], send3, recv3, d).start()

    in3[slab] = out3[slab]

    send_tiles(1)

    pick = jnp.where(
        lax.broadcasted_iota(jnp.int32, (LANES, CHAN), 0) % CHAN == lax.broadcasted_iota(jnp.int32, (LANES, CHAN), 1),
        1.0,
        0.0,
    )
    by_name["local"].wait()
    mixed = exact_product(pick, local_ref[...], ((1,), (1,)))
    mixed = exact_product(mixed, pick, ((1,), (1,)))
    mix_high, mix_low = split(jnp.where(lane == row, mixed, 0.0))
    mix_rows = jnp.concatenate([mix_high, mix_high], axis=1)
    mix_more = jnp.concatenate([mix_low, jnp.zeros_like(mix_low)], axis=1)
    mix[...] = jnp.concatenate([mix_rows, mix_more], axis=0)

    @pl.loop(0, ROWS, unroll=4)
    def _(y):
        both = product(mix[...], jnp.concatenate([g_high[y], g_low[y]], axis=0))
        local_part[y] = both[:LANES] + both[LANES:]


    sums_a[pencil] = sums_mine[...]
    for j in range(1, PENCILS):
        d = (pencil + j) % PENCILS
        to_pencil(sums_mine, sums_a.at[d], asend, arecv.at[d], d).wait_recv()
    total = jnp.zeros((8, LANES), F32)
    for d in range(PENCILS):
        total = total + sums_a[d]
    sums_y[my_y] = total
    for j in range(1, 4):
        to_slab(sums_y.at[my_y], sums_y.at[my_y], ysend, yrecv, my_z * 4 + (my_y + j) % 4).start()

    def back_copy(half, p, to, sem):
        return to_pencil(out4.at[spans[half]], in4.at[p, spans[half]], sem, recv4.at[p, half], to)

    to_slab(out3.at[pl.ds(0, SLABS - 1)], in3.at[pl.ds(0, SLABS - 1)], send3, recv3, slab).wait_recv()
    for half, ks in enumerate((range(FIRST), range(FIRST, HALF))):
        for k in ks:
            out4[k] = in3[k] + in3[MODES - k] if 0 < k < 16 else in3[k]

        @pl.when(pencil == 0)
        def _():
            for k in ks:
                for part in range(2):
                    r = 3 + 4 * part
                    if k > 0:
                        edge4[2 * k + part : 2 * k + part + 1] = in3[MODES - k, r : r + 1]
                        out4[k, r : r + 1] = in3[k, r : r + 1] if k < 16 else jnp.zeros((1, LANES), F32)

        for j in (2, 1, 3):
            x = (chip + j) % CHIPS
            back_copy(half, pencil, x * CORES + core, send4.at[half]).start()
        back_copy(half, pencil, other, send4.at[2]).start()

    @pl.when(pencil == 0)
    def _():
        edge4[0:2] = jnp.zeros((2, LANES), F32)
        edge4[34:40] = jnp.zeros((6, LANES), F32)

        @pl.loop(1, PENCILS)
        def _(d):
            to_pencil(edge4, edge4, xsend, xrecv, d).start()

    in4[pencil] = out4[...]

    upper = modes_of(1, ei[...])
    real, imag = both_parts(upper)
    grads[...] = (low_modes[0] * real + low_modes[1] * imag).reshape(MODES, 16, LANES)

    @pl.loop(1, PENCILS)
    def _(j):
        d = (pencil + j) % PENCILS
        to_pencil(grads.at[pl.ds(4 * d, 2)], grad_hbm.at[pl.ds(2 * pencil, 2)], gsend, grecv, d).start()

        @pl.when(pencil != 0)
        def _():
            to_pencil(
                grads.at[pl.ds(4 * d + 2, 2)], grad_hbm.at[pl.ds(31 - 2 * pencil, 2)], gsend, grecv, d
            ).start()

        @pl.when(pencil == 0)
        def _():
            to_pencil(grads.at[4 * d + 2], grad_hbm.at[31], gsend, grecv, d).start()
            to_pencil(grads.at[4 * d + 3], grad_hbm.at[16], gsend, grecv, d).start()

    for q in range(4):
        pltpu.make_async_copy(grads.at[4 * pencil + q], grad_hbm.at[y_index(pencil, q)], own_sem.at[4 + q]).start()

    to_slab(sums_y.at[pl.ds(0, 3)], sums_y.at[pl.ds(0, 3)], ysend, yrecv, slab).wait_recv()
    total = sums_y[0]
    for j in range(1, 4):
        total = total + sums_y[j]
    sums_z[my_z] = total
    for j in range(1, 8):
        to_slab(sums_z.at[my_z], sums_z.at[my_z], zsend, zrecv, (my_z + j) % 8 * 4 + my_y).start()

    for half in range(2):
        for j in (1, 3, 2):
            d = (chip + j) % CHIPS * CORES + core
            back_copy(half, d, d, send4.at[half]).wait_recv()
            to_pencil(
                in4.at[d, spans[half]], in4.at[d, spans[half]], fsend.at[half], recv4.at[d, half], other
            ).start()

    @pl.when(pencil != 0)
    def _():
        to_pencil(edge4, edge4, xsend, xrecv, 0).wait_recv()

    spread_y[pl.ds(2 * HALF * ROWS, (XROWS - 2 * HALF) * ROWS), :] = jnp.zeros(((XROWS - 2 * HALF) * ROWS, LANES), F32)
    for half, ks in enumerate((range(FIRST), range(FIRST, HALF))):
        for x in range(CHIPS):
            back_copy(half, x * CORES + 1 - core, other, send4.at[2]).wait_recv()
        for first in range(ks.start, ks.stop, 2):
            group = range(first, min(first + 2, ks.stop))
            columns = [jnp.concatenate([in4[p, k] for p in range(PENCILS)], axis=0) for k in group]
            both = product(yi[...], stacked(jnp.concatenate(columns, axis=1)))
            for k in group:
                field = both[:, (k - first) * LANES : (k - first + 1) * LANES]
                edge_real, edge_imag = edge4[2 * k : 2 * k + 1], edge4[2 * k + 1 : 2 * k + 2]
                spread_y[k * ROWS : (k + 1) * ROWS] = field[:ROWS] + ye[0] * edge_real - ye[1] * edge_imag
                spread_y[(HALF + k) * ROWS : (HALF + k + 1) * ROWS] = (
                    field[ROWS:] + ye[0] * edge_imag + ye[1] * edge_real
                )

    to_slab(sums_z.at[pl.ds(0, 7)], sums_z.at[pl.ds(0, 7)], zsend, zrecv, slab).wait_recv()
    total = sums_z[0]
    for j in range(1, 8):
        total = total + sums_z[j]
    sums_all[...] = total * float(GRID) ** -1.5
    stores = [pltpu.make_async_copy(sums_all, sum_hbm, store_sem.at[chunks])]
    stores[0].start()

    for c in range(chunks):

        columns = []
        for r in range(CHUNK):
            value = spread_y[pl.ds(c * CHUNK + r, XROWS, stride=ROWS), :]
            high = value.astype(BF16).astype(F32)
            column = jnp.concatenate([high, value - high, high, jnp.zeros((8, LANES), F32)], axis=0)
            columns.append(column.T.astype(BF16))
        fields = product(jnp.concatenate(columns, axis=0), xi[...])
        for r in range(CHUNK):
            y = c * CHUNK + r
            result[y] = (local_part[y] + fields[r * LANES : (r + 1) * LANES]).astype(BF16)

        rows = pl.ds(c * CHUNK, CHUNK)
        stores.append(pltpu.make_async_copy(result.at[rows], result_hbm.at[rows], store_sem.at[c]))
        stores[-1].start()

    to_pencil(weights.at[pl.ds(0, 28)], weights.at[pl.ds(0, 28)], wsend, wrecv, pencil).wait_send()
    for t in range(2):
        to_pencil(out1.at[t, 1 - core], pair_in.at[t], psend.at[t], precv.at[t, 0], other).wait_send()
        for half in range(2):
            some = in1.at[t, pl.ds(0, 3), spans[half]]
            to_pencil(some, some, send1.at[t, half], recv1.at[t, 0, half], other).wait_send()
        most = pl.ds(0, SLABS - 1)
        to_slab(out2.at[t, most], in2.at[t, most], send2.at[t], recv2.at[t], slab).wait_send()

        @pl.when((core == 0) & (chip != 0))
        def _():
            to_pencil(
                sum1.at[t, pl.ds(EDGE, BLOCK - EDGE)], edge_in.at[t, chip], esend.at[t], erecv.at[t, chip], 0
            ).wait_send()

    to_pencil(sums_a.at[pl.ds(0, 7)], sums_a.at[pl.ds(0, 7)], asend, arecv.at[0], pencil).wait_send()
    to_slab(sums_y.at[pl.ds(0, 3)], sums_y.at[pl.ds(0, 3)], ysend, yrecv, slab).wait_send()
    to_slab(sums_z.at[pl.ds(0, 7)], sums_z.at[pl.ds(0, 7)], zsend, zrecv, slab).wait_send()
    to_slab(out3.at[pl.ds(0, 31)], in3.at[pl.ds(0, 31)], send3, recv3, slab).wait_send()
    for half in range(2):
        some = in4.at[pl.ds(0, 3), spans[half]]
        to_pencil(some, some, send4.at[half], recv4.at[0, half], other).wait_send()
        to_pencil(some, some, fsend.at[half], recv4.at[0, half], other).wait_send()
    to_pencil(out4, in4.at[pencil], send4.at[2], recv4.at[pencil, 0], other).wait_send()

    @pl.when(pencil == 0)
    def _():
        for d in range(1, PENCILS):
            to_pencil(edge4, edge4, xsend, xrecv, d).wait_send()

    to_pencil(grads.at[pl.ds(0, 28)], grad_hbm.at[pl.ds(0, 28)], gsend, grecv, pencil).wait()
    for q in range(4):
        pltpu.make_async_copy(grads.at[4 * pencil + q], grad_hbm.at[y_index(pencil, q)], own_sem.at[4 + q]).wait()
    for store in stores:
        store.wait()


def last_kernel(
    result_hbm, grad_in, sum_hbm,
    out_hbm, local_hbm, grad_out,
    result, grad, sum_ref, local_ref, load_sem, store_sem,
):
    rows = [pl.ds(c * (ROWS // PARTS), ROWS // PARTS) for c in range(PARTS)]
    loads = [pltpu.make_async_copy(result_hbm.at[r], result.at[r], load_sem.at[c]) for c, r in enumerate(rows)]
    stores = [pltpu.make_async_copy(result.at[r], out_hbm.at[r], store_sem.at[c]) for c, r in enumerate(rows)]
    loads.append(pltpu.make_async_copy(grad_in, grad, load_sem.at[PARTS]))
    stores.append(pltpu.make_async_copy(grad, grad_out, store_sem.at[PARTS]))
    load_sum = pltpu.make_async_copy(sum_hbm, sum_ref, load_sem.at[PARTS + 1])
    load_sum.start()
    for load in loads:
        load.start()

    o_row = lax.broadcasted_iota(jnp.int32, (CHAN, LANES), 0)
    o_lane = lax.broadcasted_iota(jnp.int32, (CHAN, LANES), 1)
    load_sum.wait()
    total = jnp.where(o_row < 8, sum_ref[0:1], sum_ref[1:2])
    total = jnp.where(o_row % 8 == o_lane // CHAN, total, 0.0)
    pick = jnp.where(
        lax.broadcasted_iota(jnp.int32, (LANES, CHAN), 0) % CHAN == lax.broadcasted_iota(jnp.int32, (LANES, CHAN), 1),
        1.0,
        0.0,
    )
    local_ref[...] = exact_product(total, pick, ((1,), (0,)))
    store_local = pltpu.make_async_copy(local_ref, local_hbm, store_sem.at[PARTS + 1])
    store_local.start()
    for load, store in zip(loads, stores):
        load.wait()
        store.start()
    for store in stores:
        store.wait()
    store_local.wait()


def on_device(activation, preact, cotangent, local_weight, spectral_weight):
    made = tables()
    fields = [a.reshape(ROWS, LANES, GRID) for a in (activation, preact, cotangent)]
    weight = spectral_weight[0].reshape(MODES, 4, 2, 2, LANES).transpose(0, 1, 3, 2, 4).reshape(MODES, 16, LANES)
    any_space = pl.BlockSpec(memory_space=pl.ANY)
    dma = pltpu.SemaphoreType.DMA
    field = pltpu.VMEM((ROWS, LANES, GRID), BF16)
    wide_field = pltpu.VMEM((ROWS, LANES, GRID), F32)
    tile = (8, LANES)
    result, grad, total = pl.pallas_call(
        modes_kernel,
        out_shape=(
            jax.ShapeDtypeStruct((ROWS, LANES, GRID), BF16),
            jax.ShapeDtypeStruct((MODES, 16, LANES), F32),
            jax.ShapeDtypeStruct(tile, F32),
        ),
        in_specs=[any_space] * (5 + len(TABLE_NAMES)),
        out_specs=(any_space, any_space, any_space),
        scratch_shapes=[
            field, field, field, field, field, wide_field, field,
            pltpu.VMEM((2 * GRID, LANES), BF16),
            pltpu.VMEM((80, 192), BF16),
            pltpu.VMEM((2, MODE_ROWS, 256), BF16),
            pltpu.VMEM((2, 256, MODE_ROWS), BF16),
            pltpu.VMEM((2, MODE_ROWS // 8, 8, LANES), F32),
            pltpu.VMEM((256, 256), BF16),
            pltpu.VMEM((256, 256), BF16),
            pltpu.VMEM((256, LANES), BF16),
            pltpu.VMEM((64, 192), BF16),
            pltpu.VMEM((2, ROWS, LANES), F32),
            pltpu.VMEM((128, GRID), BF16),
            pltpu.VMEM((2, ROWS * XROWS, LANES), F32),
            pltpu.VMEM((ROWS * XROWS, LANES), F32),
            pltpu.VMEM((2, CORES, BLOCK) + tile, F32),
            pltpu.VMEM((2, BLOCK) + tile, F32),
            pltpu.VMEM((2, BLOCK) + tile, F32),
            pltpu.VMEM((2, CHIPS, HALF) + tile, F32),
            pltpu.VMEM((2, CHIPS, BLOCK - EDGE) + tile, F32),
            pltpu.VMEM((2, SLABS) + tile, F32),
            pltpu.VMEM((2, SLABS) + tile, F32),
            pltpu.VMEM((MODES, 16, LANES), F32),
            pltpu.VMEM((2, MODE_ROWS // 8, 8, LANES), F32),
            pltpu.VMEM((2, MODE_ROWS // 8, 8, LANES), F32),
            pltpu.VMEM((SLABS,) + tile, F32),
            pltpu.VMEM((SLABS,) + tile, F32),
            pltpu.VMEM((HALF,) + tile, F32),
            pltpu.VMEM((PENCILS, HALF) + tile, F32),
            pltpu.VMEM((XROWS, LANES), F32),
            pltpu.VMEM((MODES, 16, LANES), F32),
            pltpu.VMEM((2 * LANES, LANES), F32),
            pltpu.VMEM((PENCILS,) + tile, F32),
            pltpu.VMEM((4,) + tile, F32),
            pltpu.VMEM((8,) + tile, F32),
            pltpu.VMEM(tile, F32),
            pltpu.VMEM(tile, F32),
            pltpu.VMEM((CHAN, CHAN), F32),
            pltpu.VMEM((2 * LANES, 2 * LANES), BF16),
            dma((len(TABLE_NAMES) + 1,)), dma((3, len(LOADS))), dma((ROWS // CHUNK + 1,)), dma((8,)),
            dma((2,)), dma((2, 2)), dma((2, 2)), dma((2, CHIPS, 2)), dma((2,)), dma((2, CHIPS)),
            dma((2,)), dma((2,)), dma, dma,
            dma, dma, dma((3,)), dma((PENCILS, 2)), dma((2,)), dma, dma, dma, dma,
            dma, dma((PENCILS,)), dma, dma, dma, dma,
        ],
        compiler_params=pltpu.CompilerParams(
            collective_id=0, has_side_effects=True, vmem_limit_bytes=62 * 1024 * 1024
        ),
        cost_estimate=pl.CostEstimate(flops=3_000_000_000, bytes_accessed=11_000_000, transcendentals=2_000_000),
        name="modes",
    )(*fields, weight, local_weight, *(jnp.asarray(made[name]) for name in TABLE_NAMES))
    out, grad_local, grad_spectral = pl.pallas_call(
        last_kernel,
        out_shape=(
            jax.ShapeDtypeStruct((ROWS, LANES, GRID), BF16),
            jax.ShapeDtypeStruct((CHAN, CHAN), F32),
            jax.ShapeDtypeStruct((MODES, 16, LANES), F32),
        ),
        in_specs=[any_space, any_space, any_space],
        out_specs=(any_space, any_space, any_space),
        scratch_shapes=[
            field,
            pltpu.VMEM((MODES, 16, LANES), F32),
            pltpu.VMEM(tile, F32),
            pltpu.VMEM((CHAN, CHAN), F32),
            dma((PARTS + 2,)), dma((PARTS + 2,)),
        ],
        compiler_params=pltpu.CompilerParams(vmem_limit_bytes=62 * 1024 * 1024),
        cost_estimate=pl.CostEstimate(flops=100_000, bytes_accessed=5_000_000, transcendentals=0),
        name="last",
    )(result, grad, total)
    grad_spectral = grad_spectral.reshape(MODES, 4, 2, 2, LANES).transpose(0, 1, 3, 2, 4).reshape(spectral_weight.shape)
    return out.reshape(activation.shape), grad_local, grad_spectral


def solution(mesh):
    field = P("pencil", "slab", None, None)
    modes = P("slab", None, "pencil", None, None)
    return jax.shard_map(
        on_device,
        mesh=mesh,
        in_specs=(field, field, field, P(), modes),
        out_specs=(field, P(), modes),
        check_vma=False,
    )
```
